32 devices in a mesh: dp: 2 (over y), expert: 16 (over z, x, core).
Axes of the slice: x: 2, y: 2, z: 4, core: 2. Of those that a mesh axis runs over, the one named last changes fastest.
Arguments:
- tokens: bfloat16 [128, 4096], P('expert', 'dp'), may hold values from -6 to 6
- expert_ids: int32 [128, 8], P('expert'), may hold values from 0 to 15, all different within a row; in each aligned block of 8 rows (0 to 7, 8 to 15, ...) at most 8 rows name the same one
- route_weights: float32 [128, 8], P('expert'), may hold values from 0.2 to 1
- w_gate: bfloat16 [16, 4096, 768], P('expert', 'dp'), may hold values from -0.09375 to 0.09375
- w_up: bfloat16 [16, 4096, 768], P('expert', 'dp'), may hold values from -0.09375 to 0.09375
- w_down: bfloat16 [16, 768, 4096], P('expert', None, 'dp'), may hold values from -0.21875 to 0.21875
- grad_out: bfloat16 [128, 4096], P('expert', 'dp'), may hold values from -6 to 6
Outputs:
- layer_out: bfloat16 [128, 4096], P('expert', 'dp')
- input_grad: bfloat16 [128, 4096], P('expert', 'dp')
- gate_weight_grad: bfloat16 [16, 4096, 768], P('expert', 'dp')
- up_weight_grad: bfloat16 [16, 4096, 768], P('expert', 'dp')
- down_weight_grad: bfloat16 [16, 768, 4096], P('expert', None, 'dp')
The draws below stay inside these ranges and needn't reach their ends.
Inputs may be any that keep to these rules, and one draw needn't show every extreme that they name: `expert_ids`: among the 8 tokens of one block no expert is named more than 8 times, and in some block some expert is named exactly 8 times; a token names 8 different experts.
All inputs are finite; a program needn't handle non-finite values.
Results may differ from the reference program's by a relative error of at most 0.028.
Values may be sent and summed in bfloat16 or wider, within the bound.
A program may use at most 64 MiB of HBM per device.

```python
import math
import jax
import jax.numpy as jnp
import numpy as np
from jax import lax

MODEL_WIDTH = 4096
FF = 768
CHOSEN_EXPERTS = 8
TOKENS_PER_SHARD = 8
EXPERTS = 16
CAP = 8
TOKENS = 128
N_DP = 2
N_EXPERT = 16


def levels(own_key, extent, cuts, low, top_value):
    def one(position, parts):
        draws = jax.random.uniform(jax.random.fold_in(jax.random.fold_in(own_key, 6), position), (parts,), jnp.float32, low / len(cuts), top_value / len(cuts))
        return jnp.repeat(jnp.exp(draws), extent[position] // parts).reshape((-1,) + (1,) * (len(extent) - position - 1))

    factor_of = one(*cuts[0])
    for cut in cuts[1:]:
        factor_of = factor_of * one(*cut)
    return factor_of


def assign_block(stream_key, own, number, rows, count, top, reach, skew):
    order = jax.random.permutation(stream_key, count)
    crowded, usual = load_shares(count, rows * top, reach, skew, True), load_shares(count, rows * top, reach, skew, False)
    places = jnp.arange(count)

    def named(tallies, turn):
        used = int((tallies > 0).sum())
        fixed = max(1, used // 4)
        moved = fixed + (places - fixed + turn * (used - fixed)) % max(1, count - fixed)
        return jnp.zeros((count,), jnp.int32).at[order[jnp.where(places < fixed, places, moved)]].set(jnp.asarray(tallies, jnp.int32))

    tallies = jnp.where(number % 4 == 0, named(crowded, number // 4), named(usual, number - number // 4 - 1))
    mixed = jax.random.permutation(jax.random.fold_in(own, 3), count)
    giver, receiver = mixed[0:count // 2 * 2:2], mixed[1:count // 2 * 2:2]
    slack = jnp.minimum(tallies[giver] - 1, reach - tallies[receiver]) // 2
    slack = jnp.where((giver == order[0]) | (receiver == order[0]) | (tallies[receiver] == 0), 0, jnp.maximum(slack, 0))
    moved = jax.random.randint(jax.random.fold_in(own, 4), (count // 2,), 0, 1 << 20) % (slack + 1)
    tallies = tallies.at[giver].add(-moved).at[receiver].add(moved)
    items = jnp.searchsorted(jnp.cumsum(tallies), jnp.arange(rows * top), side="right").astype(jnp.int32)
    grid = items.reshape(top, rows).T
    grid = grid[jax.random.permutation(jax.random.fold_in(own, 1), rows)]
    turn = jax.random.randint(jax.random.fold_in(own, 2), (rows, 1), 0, top)
    return jnp.take_along_axis(grid, (jnp.arange(top)[None, :] + turn) % top, axis=1)


def load_shares(amount, total, most, lean, full):
    loads = [(1 << 20) // math.isqrt(standing ** lean) + 1 for standing in range(1, amount + 1)]
    largest = most if full else min(most, max(-(-total // amount), total * loads[0] // sum(loads)))
    least = 1 if total - largest >= amount - 1 else 0
    counts, rest = [largest] + [least] * (amount - 1), total - largest - least * (amount - 1)
    while rest > 0:
        movable = [i for i in range(1, amount) if counts[i] < largest] or [i for i in range(1, amount) if counts[i] < most]
        whole, left = sum([loads[i] for i in movable]), rest
        for i in movable:
            addition = min(most - counts[i], max(1, left * loads[i] // whole), rest)
            counts[i] = counts[i] + addition
            rest = rest - addition
    return np.array(counts)


def gaussian(own_key, shape, scale, most, split=(), held_as=jnp.bfloat16):
    entries = scale * jax.random.normal(own_key, shape, jnp.float32)
    if split:
        entries = entries * levels(own_key, shape, split, -0.22, 0.18)
    return jnp.clip(entries, -most, most).astype(held_as)


def setup_inputs(seed: int = 0) -> dict:
    arg_keys = jax.random.split(jax.random.key(seed), 8)
    tokens = gaussian(arg_keys[0], (TOKENS, MODEL_WIDTH), 1.0, 6.0, ((0, 16), (1, 2)))
    expert_ids_keys = jax.random.split(jax.random.fold_in(arg_keys[1], 1), TOKENS // TOKENS_PER_SHARD)
    expert_ids_turns = jax.random.permutation(jax.random.fold_in(arg_keys[1], 3), TOKENS // TOKENS_PER_SHARD)
    expert_ids = jax.vmap(lambda own, number: assign_block(jax.random.fold_in(arg_keys[1], 2), own, number, TOKENS_PER_SHARD, EXPERTS, CHOSEN_EXPERTS, CAP, 1))(expert_ids_keys, expert_ids_turns).reshape((TOKENS, CHOSEN_EXPERTS))
    route_weights = jnp.clip(0.2 + 0.8 * jax.random.uniform(arg_keys[2], (TOKENS, CHOSEN_EXPERTS), jnp.float32) ** levels(arg_keys[2], (TOKENS, CHOSEN_EXPERTS), ((0, 16),), -0.2, 0.2), 0.2, 1.0)
    w_gate = gaussian(arg_keys[3], (EXPERTS, MODEL_WIDTH, FF), MODEL_WIDTH ** -0.5, 0.09375, ((0, 16), (1, 2)))
    w_up = gaussian(arg_keys[4], (EXPERTS, MODEL_WIDTH, FF), MODEL_WIDTH ** -0.5, 0.09375, ((0, 16), (1, 2)))
    w_down = gaussian(arg_keys[5], (EXPERTS, FF, MODEL_WIDTH), FF ** -0.5, 0.21875, ((0, 16), (2, 2)))
    grad_out = gaussian(arg_keys[6], (TOKENS, MODEL_WIDTH), 1.0, 6.0, ((0, 16), (1, 2)))
    return dict(tokens=tokens, expert_ids=expert_ids, route_weights=route_weights, w_gate=w_gate, w_up=w_up, w_down=w_down, grad_out=grad_out)


def slot_table(id_block, experts, capacity):
    flat_ids = id_block.reshape(-1).astype(jnp.int32)
    onehot = (flat_ids[:, None] == jnp.arange(experts, dtype=jnp.int32)[None, :]).astype(jnp.int32)
    before = jnp.cumsum(onehot, axis=0) - onehot
    slot_index = jnp.sum(before * onehot, axis=1)
    target = flat_ids * capacity + slot_index
    row_index = jnp.arange(experts * capacity, dtype=jnp.int32)
    return (row_index[:, None] == target[None, :]).astype(jnp.bfloat16)


def block_sum(form, left, right):
    products = jnp.einsum(form, left, right)
    rounded = lax.optimization_barrier(products.astype(jnp.bfloat16))
    return jnp.sum(rounded.astype(jnp.float32), axis=0)


def gate_grads(hidden_grad, gate, up_value):
    sigmoid_gate = jax.nn.sigmoid(gate)
    silu_gate = gate * sigmoid_gate
    gate_grad = (hidden_grad * up_value * sigmoid_gate * (1.0 + gate * (1.0 - sigmoid_gate))).astype(jnp.bfloat16)
    up_grad = (hidden_grad * silu_gate).astype(jnp.bfloat16)
    return gate_grad, up_grad


def expert_pass(packed):
    expert_in, expert_grad, gate_matrix, up_matrix, down_matrix = packed
    slices = MODEL_WIDTH // N_DP
    row_count = expert_in.shape[0]
    in_blocks = expert_in.astype(jnp.float32).reshape(row_count, N_DP, slices)
    gate = block_sum("rbd,bdf->brf", in_blocks, gate_matrix.astype(jnp.float32).reshape(N_DP, slices, FF))
    up_value = block_sum("rbd,bdf->brf", in_blocks, up_matrix.astype(jnp.float32).reshape(N_DP, slices, FF))
    hidden = (gate * jax.nn.sigmoid(gate) * up_value).astype(jnp.bfloat16)
    expert_out = jnp.dot(hidden, down_matrix, preferred_element_type=jnp.float32).astype(jnp.bfloat16)
    grad_blocks = expert_grad.astype(jnp.float32).reshape(row_count, N_DP, slices)
    hidden_grad = block_sum("rbd,fbd->brf", grad_blocks, down_matrix.astype(jnp.float32).reshape(FF, N_DP, slices))
    gate_grad, up_grad = gate_grads(hidden_grad, gate, up_value)
    down_grad = jnp.dot(hidden.T, expert_grad, preferred_element_type=jnp.float32).astype(jnp.bfloat16)
    gate_weight = jnp.dot(expert_in.T, gate_grad, preferred_element_type=jnp.float32).astype(jnp.bfloat16)
    up_weight = jnp.dot(expert_in.T, up_grad, preferred_element_type=jnp.float32).astype(jnp.bfloat16)
    input_rows = (jnp.dot(gate_grad, gate_matrix.T, preferred_element_type=jnp.float32)
                  + jnp.dot(up_grad, up_matrix.T, preferred_element_type=jnp.float32)).astype(jnp.bfloat16)
    return expert_out, input_rows, gate_weight, up_weight, down_grad


def to_sources(rows):
    return rows.reshape(EXPERTS, N_EXPERT, CAP, MODEL_WIDTH).transpose(1, 0, 2, 3).reshape(N_EXPERT, EXPERTS * CAP, MODEL_WIDTH)


def reference(tokens, expert_ids, route_weights, w_gate, w_up, w_down, grad_out):
    id_blocks = expert_ids.reshape(N_EXPERT, TOKENS_PER_SHARD, CHOSEN_EXPERTS)
    tables = jax.vmap(lambda id_block: slot_table(id_block, EXPERTS, CAP))(id_blocks)
    slot_table_float = tables.astype(jnp.float32)
    weight_rep = route_weights.reshape(N_EXPERT, TOKENS_PER_SHARD * CHOSEN_EXPERTS)
    token_replicas = jnp.repeat(tokens.reshape(N_EXPERT, TOKENS_PER_SHARD, MODEL_WIDTH), CHOSEN_EXPERTS, axis=1).astype(jnp.float32)
    gradient_rounding = (jnp.repeat(grad_out.reshape(N_EXPERT, TOKENS_PER_SHARD, MODEL_WIDTH), CHOSEN_EXPERTS, axis=1).astype(jnp.float32)
                  * weight_rep[:, :, None]).astype(jnp.bfloat16)
    gradient_rounding = lax.optimization_barrier(gradient_rounding)
    dispatch_token_rows = jnp.einsum("euc,ecg->eug", slot_table_float, token_replicas).astype(jnp.bfloat16)
    dispatch_gradients = jnp.einsum("euc,ecg->eug", slot_table_float, gradient_rounding.astype(jnp.float32)).astype(jnp.bfloat16)
    expert_in = dispatch_token_rows.reshape(N_EXPERT, EXPERTS, CAP, MODEL_WIDTH).transpose(1, 0, 2, 3).reshape(EXPERTS, N_EXPERT * CAP, MODEL_WIDTH)
    expert_grad = dispatch_gradients.reshape(N_EXPERT, EXPERTS, CAP, MODEL_WIDTH).transpose(1, 0, 2, 3).reshape(EXPERTS, N_EXPERT * CAP, MODEL_WIDTH)
    results = lax.map(expert_pass, (expert_in, expert_grad, w_gate, w_up, w_down))
    output_row_block = to_sources(results[0]).astype(jnp.float32)
    gradient_row_block = to_sources(results[1]).astype(jnp.float32)
    backward_output = jnp.einsum("pat,paz->ptz", slot_table_float, output_row_block).reshape(N_EXPERT, TOKENS_PER_SHARD, CHOSEN_EXPERTS, MODEL_WIDTH)
    backward_input = jnp.einsum("pat,paz->ptz", slot_table_float, gradient_row_block).reshape(N_EXPERT, TOKENS_PER_SHARD, CHOSEN_EXPERTS, MODEL_WIDTH)
    weights_full = route_weights.reshape(N_EXPERT, TOKENS_PER_SHARD, CHOSEN_EXPERTS)
    layer_out = jnp.sum(backward_output * weights_full[:, :, :, None], axis=2).astype(jnp.bfloat16).reshape(TOKENS, MODEL_WIDTH)
    input_grad = jnp.sum(backward_input, axis=2).astype(jnp.bfloat16).reshape(TOKENS, MODEL_WIDTH)
    return layer_out, input_grad, results[2], results[3], results[4]
```

```python
import functools

import jax
import jax.numpy as jnp
from jax import lax
from jax.experimental import pallas as pl
from jax.experimental.pallas import tpu as pltpu
from jax.sharding import PartitionSpec as P

MESH = pl.DeviceIdType.MESH
LANES = 128


def slot_table(id_block, experts, capacity):
    flat_ids = id_block.reshape(-1)
    onehot = (flat_ids[:, None] == jnp.arange(experts, dtype=jnp.int32)[None, :]).astype(jnp.int32)
    before = jnp.cumsum(onehot, axis=0) - onehot
    slot_index = jnp.sum(before * onehot, axis=1)
    target = flat_ids * capacity + slot_index
    row_index = jnp.arange(experts * capacity, dtype=jnp.int32)
    return (row_index[:, None] == target[None, :]).astype(jnp.bfloat16)


def gate_grads(hidden_grad, gate, up_value):
    sigmoid_gate = jax.nn.sigmoid(gate)
    silu_gate = gate * sigmoid_gate
    gate_grad = (
        hidden_grad * up_value * sigmoid_gate * (1.0 + gate * (1.0 - sigmoid_gate))
    ).astype(jnp.bfloat16)
    up_grad = (hidden_grad * silu_gate).astype(jnp.bfloat16)
    return (gate_grad, up_grad)


def contract_rows(left, right):
    return lax.dot_general(
        left, right, (((0,), (0,)), ((), ())), preferred_element_type=jnp.float32
    )


def contract_cols(left, right):
    return lax.dot_general(
        left, right, (((1,), (1,)), ((), ())), preferred_element_type=jnp.float32
    )


def general(tokens, expert_ids, route_weights, w_gate, w_up, w_down, grad_out):
    tok_rows = tokens.shape[0]
    slices = tokens.shape[1]
    top_count = expert_ids.shape[1]
    experts = lax.axis_size("expert")
    capacity = min(tok_rows, 3 * tok_rows * top_count // experts)
    table = slot_table(expert_ids, experts, capacity)
    weight_flat = route_weights.reshape(-1)
    token_replicas = jnp.repeat(tokens, top_count, axis=0)
    grad_rep = (
        jnp.repeat(grad_out, top_count, axis=0).astype(jnp.float32) * weight_flat[:, None]
    ).astype(jnp.bfloat16)
    dispatch_token_rows = jnp.dot(table, token_replicas, preferred_element_type=jnp.float32).astype(
        jnp.bfloat16
    )
    dispatch_gradients = jnp.dot(table, grad_rep, preferred_element_type=jnp.float32).astype(
        jnp.bfloat16
    )
    dispatch_token_rows = dispatch_token_rows.reshape(experts, capacity, slices)
    dispatch_gradients = dispatch_gradients.reshape(experts, capacity, slices)
    expert_in, expert_grad = (
        lax.all_to_all(dispatch_token_rows, "expert", split_axis=0, concat_axis=0, tiled=True),
        lax.all_to_all(dispatch_gradients, "expert", split_axis=0, concat_axis=0, tiled=True),
    )
    expert_in = expert_in.reshape(-1, slices)
    expert_grad = expert_grad.reshape(-1, slices)
    gate_matrix = w_gate[0]
    up_matrix = w_up[0]
    down_matrix = w_down[0]
    gate_part = jnp.dot(expert_in, gate_matrix, preferred_element_type=jnp.float32)
    up_part = jnp.dot(expert_in, up_matrix, preferred_element_type=jnp.float32)
    gate, up_value = (
        lax.psum(gate_part.astype(jnp.bfloat16), "dp").astype(jnp.float32),
        lax.psum(up_part.astype(jnp.bfloat16), "dp").astype(jnp.float32),
    )
    hidden = (gate * jax.nn.sigmoid(gate) * up_value).astype(jnp.bfloat16)
    expert_out = jnp.dot(hidden, down_matrix, preferred_element_type=jnp.float32).astype(
        jnp.bfloat16
    )
    out_blocks = expert_out.reshape(experts, capacity, slices)
    grad_part = contract_cols(expert_grad, down_matrix)
    hidden_grad = lax.psum(grad_part.astype(jnp.bfloat16), "dp").astype(jnp.float32)
    gate_grad, up_grad = gate_grads(hidden_grad, gate, up_value)
    down_grad = contract_rows(hidden, expert_grad).astype(jnp.bfloat16)
    gate_weight = contract_rows(expert_in, gate_grad).astype(jnp.bfloat16)
    up_weight = contract_rows(expert_in, up_grad).astype(jnp.bfloat16)
    input_rows = (contract_cols(gate_grad, gate_matrix) + contract_cols(up_grad, up_matrix)).astype(
        jnp.bfloat16
    )
    input_blocks = input_rows.reshape(experts, capacity, slices)
    out_back, input_back = (
        lax.all_to_all(out_blocks, "expert", split_axis=0, concat_axis=0, tiled=True),
        lax.all_to_all(input_blocks, "expert", split_axis=0, concat_axis=0, tiled=True),
    )
    backward_output = contract_rows(table, out_back.reshape(-1, slices)).reshape(
        tok_rows, top_count, slices
    )
    backward_input = contract_rows(table, input_back.reshape(-1, slices)).reshape(
        tok_rows, top_count, slices
    )
    layer_out = jnp.sum(backward_output * route_weights[:, :, None], axis=1).astype(jnp.bfloat16)
    input_grad = jnp.sum(backward_input, axis=1).astype(jnp.bfloat16)
    return (layer_out, input_grad, gate_weight[None], up_weight[None], down_grad[None])


def partner(index, step):
    bit = 1
    while bit <= step:
        if step & bit:
            index = index + bit - 2 * bit * ((index // bit) % 2)
        bit *= 2
    return index


def exchange_kernel(
    planes,
    tok_ref, grad_ref, id_ref, weight_ref, gate_hbm, up_hbm, down_hbm,
    x_ref, eg_ref, hidden_ref, gg_ref, ug_ref, sum_ref,
    w_gate, w_up, w_down, load_sem,
    msg, scale, part, other, back, back_sib, mid, mid_x, last, last_z,
    z_send, z_recv, x_send, x_recv, s_send, s_recv, y_send, y_recv,
    r1_send, r1_recv, r2_send, r2_recv, r3_send, r3_recv,
):
    rows, wide = tok_ref.shape
    ff = w_gate.shape[1]
    top = id_ref.shape[1]
    chunk = 4 * rows
    me = lax.axis_index("expert")
    core = me % 2
    side = (me // 2) % 2
    plane = me // 4
    pair = {"dp": 1 - lax.axis_index("dp")}
    sibling = {"expert": plane * 4 + side * 2 + (1 - core)}
    across = {"expert": plane * 4 + (1 - side) * 2 + core}

    def in_plane(step):
        return {"expert": partner(plane, step) * 4 + side * 2 + core}

    loads = []
    for i, (source, target) in enumerate(
        ((gate_hbm, w_gate), (up_hbm, w_up), (down_hbm, w_down))
    ):
        load = pltpu.make_async_copy(source.at[0], target, load_sem.at[i])
        load.start()
        loads.append(load)

    peers = [sibling, across, pair] + [in_plane(step) for step in range(1, planes)]
    barrier = pltpu.get_barrier_semaphore()
    for peer in peers:
        pl.semaphore_signal(barrier, inc=1, device_id=peer, device_id_type=MESH)

    lane = lax.broadcasted_iota(jnp.int32, (rows, LANES), 1)
    dense = jnp.zeros((rows, LANES), jnp.float32)
    chosen = jnp.zeros((rows, LANES), jnp.float32)
    for k in range(top):
        hit = id_ref[:, k:k + 1] == lane
        dense = dense + jnp.where(hit, weight_ref[:, k:k + 1], 0.0)
        chosen = chosen + jnp.where(hit, 1.0, 0.0)
    high = dense.astype(jnp.bfloat16).astype(jnp.float32)
    middle = (dense - high).astype(jnp.bfloat16).astype(jnp.float32)
    low = dense - high - middle
    both = jnp.concatenate(
        [tok_ref[...].astype(jnp.float32), grad_ref[...].astype(jnp.float32)], axis=0
    )
    extra_a = jnp.concatenate([high, low], axis=0)
    extra_b = jnp.concatenate([middle, chosen], axis=0)
    msg[0, side, core, :, :wide] = both.astype(jnp.bfloat16)
    msg[0, side, core, :, wide:wide + LANES] = extra_a.astype(jnp.bfloat16)
    msg[0, side, core, :, wide + LANES:] = extra_b.astype(jnp.bfloat16)

    pl.semaphore_wait(barrier, len(peers))

    sends = []

    def send(source, target, send_sem, recv_sem, device):
        copy = pltpu.make_async_remote_copy(
            src_ref=source, dst_ref=target, send_sem=send_sem, recv_sem=recv_sem,
            device_id=device, device_id_type=MESH,
        )
        copy.start()
        sends.append(copy)

    def arrived(target, send_sem, recv_sem, device):
        pltpu.make_async_remote_copy(
            src_ref=target, dst_ref=target, send_sem=send_sem, recv_sem=recv_sem,
            device_id=device, device_id_type=MESH,
        ).wait_recv()

    def spread(k):
        own = msg.at[k, side, core]
        if k > 0:
            arrived(own, z_send.at[k], z_recv.at[k], in_plane(k))
        send(own, own, x_send.at[k], x_recv.at[k], across)
        send(own, own, s_send.at[k, 0], s_recv.at[k, 0], sibling)

    def relay(k):
        far = msg.at[k, 1 - side, core]
        arrived(far, x_send.at[k], x_recv.at[k], across)
        send(far, far, s_send.at[k, 1], s_recv.at[k, 1], sibling)

    def gather_end(k):
        arrived(msg.at[k, side, 1 - core], s_send.at[k, 0], s_recv.at[k, 0], sibling)
        arrived(msg.at[k, 1 - side, 1 - core], s_send.at[k, 1], s_recv.at[k, 1], sibling)

    def first_half(k):
        mine = lax.broadcasted_iota(jnp.int32, (rows, LANES), 1) == me
        at = k * chunk
        for s in range(2):
            ins, grads = [], []
            for c in range(2):
                extra = msg[k, s, c, :, wide:].astype(jnp.float32)
                dense_w = extra[:rows, :LANES] + extra[:rows, LANES:] + extra[rows:, :LANES]
                weight = jnp.sum(jnp.where(mine, dense_w, 0.0), axis=1, keepdims=True)
                mask = jnp.sum(jnp.where(mine, extra[rows:, LANES:], 0.0), axis=1, keepdims=True)
                body = msg[k, s, c, :, :wide].astype(jnp.float32)
                ins.append(body[:rows] * mask)
                grads.append(body[rows:] * weight)
                j = 2 * s + c
                scale[k, j * rows:(j + 1) * rows, :] = jnp.broadcast_to(weight, (rows, LANES))
            here = slice(at + 2 * s * rows, at + 2 * (s + 1) * rows)
            x_ref[here, :] = jnp.concatenate(ins, axis=0).astype(jnp.bfloat16)
            eg_ref[here, :] = jnp.concatenate(grads, axis=0).astype(jnp.bfloat16)

        tile = min(256, ff)
        span = slice(at, at + chunk)

        def give(i):
            send(part.at[k, i], other.at[k, i], y_send.at[k, i], y_recv.at[k, i], pair)

        for i, matrix in enumerate((w_gate, w_up)):
            if k == 0:
                loads[i].wait()

            @pl.loop(0, ff // tile)
            def _(n):
                cols = pl.ds(pl.multiple_of(n * tile, tile), tile)
                part[k, i, :, cols] = jnp.dot(
                    x_ref[span, :], matrix[:, cols], preferred_element_type=jnp.float32
                ).astype(jnp.bfloat16)

            give(i)
        if k == 0:
            loads[2].wait()

        @pl.loop(0, ff // tile)
        def _(n):
            cols = pl.ds(pl.multiple_of(n * tile, tile), tile)
            part[k, 2, :, cols] = contract_cols(eg_ref[span, :], w_down[cols, :]).astype(
                jnp.bfloat16
            )

        give(2)

    def second_half(k):
        span = slice(k * chunk, (k + 1) * chunk)
        for i in range(3):
            arrived(other.at[k, i], y_send.at[k, i], y_recv.at[k, i], pair)
        gate, up_value, hidden_grad = [
            part[k, i].astype(jnp.float32) + other[k, i].astype(jnp.float32) for i in range(3)
        ]
        sig = jax.nn.sigmoid(gate)
        silu = gate * sig
        hidden_ref[span, :] = (silu * up_value).astype(jnp.bfloat16)
        gg_ref[span, :] = (
            hidden_grad * up_value * sig * (1.0 + gate * (1.0 - sig))
        ).astype(jnp.bfloat16)
        ug_ref[span, :] = (hidden_grad * silu).astype(jnp.bfloat16)
        tile = min(512, wide)

        @pl.loop(0, wide // tile)
        def _(n):
            cols = pl.ds(pl.multiple_of(n * tile, tile), tile)
            out = jnp.dot(
                hidden_ref[span, :], w_down[:, cols], preferred_element_type=jnp.float32
            ) * scale[k, :, 0:1]
            back_in = contract_cols(gg_ref[span, :], w_gate[cols, :]) + contract_cols(
                ug_ref[span, :], w_up[cols, :]
            )
            for s in range(2):
                for c in range(2):
                    block = slice((2 * s + c) * rows, (2 * s + c + 1) * rows)
                    back[k, c, s, :, cols] = jnp.concatenate(
                        [out[block], back_in[block]], axis=0
                    ).astype(jnp.bfloat16)

        send(back.at[k, 1 - core], back_sib.at[k], r1_send.at[k], r1_recv.at[k], sibling)

    def sum_core(k):
        arrived(back_sib.at[k], r1_send.at[k], r1_recv.at[k], sibling)
        mid[k] = (
            back[k, core].astype(jnp.float32) + back_sib[k].astype(jnp.float32)
        ).astype(jnp.bfloat16)
        send(mid.at[k, 1 - side], mid_x.at[k], r2_send.at[k], r2_recv.at[k], across)

    def sum_side(k):
        arrived(mid_x.at[k], r2_send.at[k], r2_recv.at[k], across)
        last[k] = (
            mid[k, side].astype(jnp.float32) + mid_x[k].astype(jnp.float32)
        ).astype(jnp.bfloat16)
        if k > 0:
            send(last.at[k], last_z.at[k], r3_send.at[k], r3_recv.at[k], in_plane(k))

    own = msg.at[0, side, core]
    spread(0)
    for k in range(1, planes):
        send(own, msg.at[k, side, core], z_send.at[k], z_recv.at[k], in_plane(k))

    ahead = min(2, planes - 1)
    for k in range(planes + ahead):
        if k < planes:
            relay(k)
            if k + 1 < planes:
                spread(k + 1)
            gather_end(k)
            first_half(k)
        done = k - ahead
        if done >= 0:
            second_half(done)
            if done >= 1:
                sum_core(done - 1)
            if done >= 2:
                sum_side(done - 2)
    if planes >= 2:
        sum_side(planes - 2)
    sum_core(planes - 1)
    sum_side(planes - 1)

    total = last[0].astype(jnp.float32)
    for k in range(1, planes):
        arrived(last_z.at[k], r3_send.at[k], r3_recv.at[k], in_plane(k))
        total = total + last_z[k].astype(jnp.float32)
    sum_ref[...] = total.astype(jnp.bfloat16)
    for copy in sends:
        copy.wait_send()


def exchange(tokens, expert_ids, route_weights, w_gate, w_up, w_down, grad_out):
    rows, wide = tokens.shape
    ff = w_gate.shape[2]
    experts = lax.axis_size("expert")
    planes = experts // 4
    total = experts * rows
    chunk = 4 * rows
    bf16 = jnp.bfloat16
    vmem = pl.BlockSpec(memory_space=pltpu.VMEM)
    hbm = pl.BlockSpec(memory_space=pl.ANY)
    dma = pltpu.SemaphoreType.DMA
    return pl.pallas_call(
        functools.partial(exchange_kernel, planes),
        out_shape=(
            jax.ShapeDtypeStruct((total, wide), bf16),
            jax.ShapeDtypeStruct((total, wide), bf16),
            jax.ShapeDtypeStruct((total, ff), bf16),
            jax.ShapeDtypeStruct((total, ff), bf16),
            jax.ShapeDtypeStruct((total, ff), bf16),
            jax.ShapeDtypeStruct((2 * rows, wide), bf16),
        ),
        in_specs=[vmem] * 4 + [hbm] * 3,
        out_specs=(vmem,) * 6,
        scratch_shapes=[
            pltpu.VMEM((wide, ff), bf16),
            pltpu.VMEM((wide, ff), bf16),
            pltpu.VMEM((ff, wide), bf16),
            dma((3,)),
            pltpu.VMEM((planes, 2, 2, 2 * rows, wide + 2 * LANES), bf16),
            pltpu.VMEM((planes, chunk, LANES), jnp.float32),
            pltpu.VMEM((planes, 3, chunk, ff), bf16),
            pltpu.VMEM((planes, 3, chunk, ff), bf16),
            pltpu.VMEM((planes, 2, 2, 2 * rows, wide), bf16),
            pltpu.VMEM((planes, 2, 2 * rows, wide), bf16),
            pltpu.VMEM((planes, 2, 2 * rows, wide), bf16),
            pltpu.VMEM((planes, 2 * rows, wide), bf16),
            pltpu.VMEM((planes, 2 * rows, wide), bf16),
            pltpu.VMEM((planes, 2 * rows, wide), bf16),
            dma((planes,)), dma((planes,)),
            dma((planes,)), dma((planes,)),
            dma((planes, 2)), dma((planes, 2)),
            dma((planes, 3)), dma((planes, 3)),
            dma((planes,)), dma((planes,)),
            dma((planes,)), dma((planes,)),
            dma((planes,)), dma((planes,)),
        ],
        compiler_params=pltpu.CompilerParams(
            collective_id=0, has_side_effects=True, vmem_limit_bytes=48 * 1024 * 1024
        ),
        name="exchange",
    )(tokens, grad_out, expert_ids, route_weights, w_gate, w_up, w_down)


def weights_kernel(x_ref, eg_ref, hidden_ref, gg_ref, ug_ref, sum_ref,
                   out_ref, in_ref, gate_ref, up_ref, down_ref):
    rows = out_ref.shape[0]
    gate_ref[0] = contract_rows(x_ref[...], gg_ref[...]).astype(jnp.bfloat16)
    up_ref[0] = contract_rows(x_ref[...], ug_ref[...]).astype(jnp.bfloat16)
    down_ref[0] = contract_rows(hidden_ref[...], eg_ref[...]).astype(jnp.bfloat16)

    @pl.when(pl.program_id(0) == 0)
    def _():
        both = sum_ref[...].astype(jnp.float32)
        out_ref[...] = both[:rows].astype(jnp.bfloat16)
        in_ref[...] = both[rows:].astype(jnp.bfloat16)


def weight_grads(x, eg, hidden, gg, ug, sums):
    total, wide = x.shape
    ff = hidden.shape[1]
    rows = sums.shape[0] // 2
    tile = min(256, wide)
    bf16 = jnp.bfloat16

    def whole(shape):
        return pl.BlockSpec(shape, lambda n: (0,) * len(shape))

    cols = pl.BlockSpec((total, tile), lambda n: (0, n))
    return pl.pallas_call(
        weights_kernel,
        grid=(wide // tile,),
        out_shape=(
            jax.ShapeDtypeStruct((rows, wide), bf16),
            jax.ShapeDtypeStruct((rows, wide), bf16),
            jax.ShapeDtypeStruct((1, wide, ff), bf16),
            jax.ShapeDtypeStruct((1, wide, ff), bf16),
            jax.ShapeDtypeStruct((1, ff, wide), bf16),
        ),
        in_specs=[cols, cols] + [whole((total, ff))] * 3 + [whole((2 * rows, wide))],
        out_specs=(
            whole((rows, wide)),
            whole((rows, wide)),
            pl.BlockSpec((1, tile, ff), lambda n: (0, n, 0)),
            pl.BlockSpec((1, tile, ff), lambda n: (0, n, 0)),
            pl.BlockSpec((1, ff, tile), lambda n: (0, 0, n)),
        ),
        compiler_params=pltpu.CompilerParams(vmem_limit_bytes=32 * 1024 * 1024),
        name="weight_grads",
    )(x, eg, hidden, gg, ug, sums)


def local(tokens, expert_ids, route_weights, w_gate, w_up, w_down, grad_out):
    experts = lax.axis_size("expert")
    planes = experts // 4
    fits = (
        lax.axis_size("dp") == 2
        and experts % 4 == 0
        and planes & (planes - 1) == 0
        and planes <= 4
        and experts <= LANES
        and tokens.shape[0] % 8 == 0
    )
    if not fits:
        return general(tokens, expert_ids, route_weights, w_gate, w_up, w_down, grad_out)
    return weight_grads(
        *exchange(tokens, expert_ids, route_weights, w_gate, w_up, w_down, grad_out)
    )


def solution(mesh):
    return jax.shard_map(
        local,
        mesh=mesh,
        in_specs=(
            P("expert", "dp"),
            P("expert", None),
            P("expert", None),
            P("expert", "dp", None),
            P("expert", "dp", None),
            P("expert", None, "dp"),
            P("expert", "dp"),
        ),
        out_specs=(
            P("expert", "dp"),
            P("expert", "dp"),
            P("expert", "dp", None),
            P("expert", "dp", None),
            P("expert", None, "dp"),
        ),
        check_vma=False,
    )
```

```python
import functools

import jax
import jax.numpy as jnp
from jax import lax
from jax.experimental import pallas as pl
from jax.experimental.pallas import tpu as pltpu
from jax.sharding import PartitionSpec as P

MESH = pl.DeviceIdType.MESH
LANES = 128


def slot_table(id_block, experts, capacity):
    flat_ids = id_block.reshape(-1)
    onehot = (flat_ids[:, None] == jnp.arange(experts, dtype=jnp.int32)[None, :]).astype(jnp.int32)
    before = jnp.cumsum(onehot, axis=0) - onehot
    slot_index = jnp.sum(before * onehot, axis=1)
    target = flat_ids * capacity + slot_index
    row_index = jnp.arange(experts * capacity, dtype=jnp.int32)
    return (row_index[:, None] == target[None, :]).astype(jnp.bfloat16)


def gate_grads(hidden_grad, gate, up_value):
    sigmoid_gate = jax.nn.sigmoid(gate)
    silu_gate = gate * sigmoid_gate
    gate_grad = (
        hidden_grad * up_value * sigmoid_gate * (1.0 + gate * (1.0 - sigmoid_gate))
    ).astype(jnp.bfloat16)
    up_grad = (hidden_grad * silu_gate).astype(jnp.bfloat16)
    return (gate_grad, up_grad)


def contract_rows(left, right):
    return lax.dot_general(
        left, right, (((0,), (0,)), ((), ())), preferred_element_type=jnp.float32
    )


def contract_cols(left, right):
    return lax.dot_general(
        left, right, (((1,), (1,)), ((), ())), preferred_element_type=jnp.float32
    )


def general(tokens, expert_ids, route_weights, w_gate, w_up, w_down, grad_out):
    tok_rows = tokens.shape[0]
    slices = tokens.shape[1]
    top_count = expert_ids.shape[1]
    experts = lax.axis_size("expert")
    capacity = min(tok_rows, 3 * tok_rows * top_count // experts)
    table = slot_table(expert_ids, experts, capacity)
    weight_flat = route_weights.reshape(-1)
    token_replicas = jnp.repeat(tokens, top_count, axis=0)
    grad_rep = (
        jnp.repeat(grad_out, top_count, axis=0).astype(jnp.float32) * weight_flat[:, None]
    ).astype(jnp.bfloat16)
    dispatch_token_rows = jnp.dot(table, token_replicas, preferred_element_type=jnp.float32).astype(
        jnp.bfloat16
    )
    dispatch_gradients = jnp.dot(table, grad_rep, preferred_element_type=jnp.float32).astype(
        jnp.bfloat16
    )
    dispatch_token_rows = dispatch_token_rows.reshape(experts, capacity, slices)
    dispatch_gradients = dispatch_gradients.reshape(experts, capacity, slices)
    expert_in, expert_grad = (
        lax.all_to_all(dispatch_token_rows, "expert", split_axis=0, concat_axis=0, tiled=True),
        lax.all_to_all(dispatch_gradients, "expert", split_axis=0, concat_axis=0, tiled=True),
    )
    expert_in = expert_in.reshape(-1, slices)
    expert_grad = expert_grad.reshape(-1, slices)
    gate_matrix = w_gate[0]
    up_matrix = w_up[0]
    down_matrix = w_down[0]
    gate_part = jnp.dot(expert_in, gate_matrix, preferred_element_type=jnp.float32)
    up_part = jnp.dot(expert_in, up_matrix, preferred_element_type=jnp.float32)
    gate, up_value = (
        lax.psum(gate_part.astype(jnp.bfloat16), "dp").astype(jnp.float32),
        lax.psum(up_part.astype(jnp.bfloat16), "dp").astype(jnp.float32),
    )
    hidden = (gate * jax.nn.sigmoid(gate) * up_value).astype(jnp.bfloat16)
    expert_out = jnp.dot(hidden, down_matrix, preferred_element_type=jnp.float32).astype(
        jnp.bfloat16
    )
    out_blocks = expert_out.reshape(experts, capacity, slices)
    grad_part = contract_cols(expert_grad, down_matrix)
    hidden_grad = lax.psum(grad_part.astype(jnp.bfloat16), "dp").astype(jnp.float32)
    gate_grad, up_grad = gate_grads(hidden_grad, gate, up_value)
    down_grad = contract_rows(hidden, expert_grad).astype(jnp.bfloat16)
    gate_weight = contract_rows(expert_in, gate_grad).astype(jnp.bfloat16)
    up_weight = contract_rows(expert_in, up_grad).astype(jnp.bfloat16)
    input_rows = (contract_cols(gate_grad, gate_matrix) + contract_cols(up_grad, up_matrix)).astype(
        jnp.bfloat16
    )
    input_blocks = input_rows.reshape(experts, capacity, slices)
    out_back, input_back = (
        lax.all_to_all(out_blocks, "expert", split_axis=0, concat_axis=0, tiled=True),
        lax.all_to_all(input_blocks, "expert", split_axis=0, concat_axis=0, tiled=True),
    )
    backward_output = contract_rows(table, out_back.reshape(-1, slices)).reshape(
        tok_rows, top_count, slices
    )
    backward_input = contract_rows(table, input_back.reshape(-1, slices)).reshape(
        tok_rows, top_count, slices
    )
    layer_out = jnp.sum(backward_output * route_weights[:, :, None], axis=1).astype(jnp.bfloat16)
    input_grad = jnp.sum(backward_input, axis=1).astype(jnp.bfloat16)
    return (layer_out, input_grad, gate_weight[None], up_weight[None], down_grad[None])


def partner(index, step):
    bit = 1
    while bit <= step:
        if step & bit:
            index = index + bit - 2 * bit * ((index // bit) % 2)
        bit *= 2
    return index


def exchange_kernel(
    planes, per,
    tok_hbm, grad_hbm, id_hbm, weight_hbm, gate_hbm, up_hbm, down_hbm,
    x_ref, eg_ref, hidden_ref, gg_ref, ug_ref, sum_ref,
    tok_ref, grad_ref, id_ref, weight_ref,
    w_gate, w_up, w_down, load_sem,
    msg, scale, part, other, back, back_sib, mid, mid_x, last, last_z,
    z_send, z_recv, x_send, x_recv, s_send, s_recv, y_send, y_recv,
    r1_send, r1_recv, r2_send, r2_recv, r3_send, r3_recv,
):
    rows, wide = tok_ref.shape
    ff = w_gate.shape[1]
    top = id_ref.shape[1]
    chunk = 4 * rows
    groups = planes // per
    held = per * chunk
    me = lax.axis_index("expert")
    core = me % 2
    side = (me // 2) % 2
    plane = me // 4
    pair = {"dp": 1 - lax.axis_index("dp")}
    sibling = {"expert": plane * 4 + side * 2 + (1 - core)}
    across = {"expert": plane * 4 + (1 - side) * 2 + core}

    def in_plane(step):
        return {"expert": partner(plane, step) * 4 + side * 2 + core}

    loads = []
    for i, (source, target) in enumerate((
        (tok_hbm, tok_ref), (grad_hbm, grad_ref), (id_hbm, id_ref), (weight_hbm, weight_ref),
        (gate_hbm.at[0], w_gate), (up_hbm.at[0], w_up), (down_hbm.at[0], w_down),
    )):
        load = pltpu.make_async_copy(source, target, load_sem.at[i])
        load.start()
        loads.append(load)

    peers = [sibling, across, pair] + [in_plane(step) for step in range(1, planes)]
    barrier = pltpu.get_barrier_semaphore()
    for peer in peers:
        pl.semaphore_signal(barrier, inc=1, device_id=peer, device_id_type=MESH)

    for load in loads[:4]:
        load.wait()
    lane = lax.broadcasted_iota(jnp.int32, (rows, LANES), 1)
    dense = jnp.zeros((rows, LANES), jnp.float32)
    chosen = jnp.zeros((rows, LANES), jnp.float32)
    for k in range(top):
        hit = id_ref[:, k:k + 1] == lane
        dense = dense + jnp.where(hit, weight_ref[:, k:k + 1], 0.0)
        chosen = chosen + jnp.where(hit, 1.0, 0.0)
    high = dense.astype(jnp.bfloat16).astype(jnp.float32)
    middle = (dense - high).astype(jnp.bfloat16).astype(jnp.float32)
    low = dense - high - middle
    both = jnp.concatenate(
        [tok_ref[...].astype(jnp.float32), grad_ref[...].astype(jnp.float32)], axis=0
    )
    extra_a = jnp.concatenate([high, low], axis=0)
    extra_b = jnp.concatenate([middle, chosen], axis=0)
    msg[0, side, core, :, :wide] = both.astype(jnp.bfloat16)
    msg[0, side, core, :, wide:wide + LANES] = extra_a.astype(jnp.bfloat16)
    msg[0, side, core, :, wide + LANES:] = extra_b.astype(jnp.bfloat16)

    pl.semaphore_wait(barrier, len(peers))

    sends = []

    def send(source, target, send_sem, recv_sem, device):
        copy = pltpu.make_async_remote_copy(
            src_ref=source, dst_ref=target, send_sem=send_sem, recv_sem=recv_sem,
            device_id=device, device_id_type=MESH,
        )
        copy.start()
        sends.append(copy)

    def arrived(target, send_sem, recv_sem, device):
        pltpu.make_async_remote_copy(
            src_ref=target, dst_ref=target, send_sem=send_sem, recv_sem=recv_sem,
            device_id=device, device_id_type=MESH,
        ).wait_recv()

    def spread(k):
        own = msg.at[k, side, core]
        if k > 0:
            arrived(own, z_send.at[k], z_recv.at[k], in_plane(k))
        send(own, own, x_send.at[k], x_recv.at[k], across)
        send(own, own, s_send.at[k, 0], s_recv.at[k, 0], sibling)

    def relay(k):
        far = msg.at[k, 1 - side, core]
        arrived(far, x_send.at[k], x_recv.at[k], across)
        send(far, far, s_send.at[k, 1], s_recv.at[k, 1], sibling)

    def gather_end(k):
        arrived(msg.at[k, side, 1 - core], s_send.at[k, 0], s_recv.at[k, 0], sibling)
        arrived(msg.at[k, 1 - side, 1 - core], s_send.at[k, 1], s_recv.at[k, 1], sibling)

    def gather_rows(k):
        mine = lax.broadcasted_iota(jnp.int32, (rows, LANES), 1) == me
        at = k * chunk
        for s in range(2):
            ins, grads = [], []
            for c in range(2):
                extra = msg[k, s, c, :, wide:].astype(jnp.float32)
                dense_w = extra[:rows, :LANES] + extra[:rows, LANES:] + extra[rows:, :LANES]
                weight = jnp.sum(jnp.where(mine, dense_w, 0.0), axis=1, keepdims=True)
                mask = jnp.sum(jnp.where(mine, extra[rows:, LANES:], 0.0), axis=1, keepdims=True)
                body = msg[k, s, c, :, :wide].astype(jnp.float32)
                ins.append(body[:rows] * mask)
                grads.append(body[rows:] * weight)
                first = at + (2 * s + c) * rows
                scale[first:first + rows, :] = jnp.broadcast_to(weight, (rows, LANES))
            here = slice(at + 2 * s * rows, at + 2 * (s + 1) * rows)
            x_ref[here, :] = jnp.concatenate(ins, axis=0).astype(jnp.bfloat16)
            eg_ref[here, :] = jnp.concatenate(grads, axis=0).astype(jnp.bfloat16)

    def first_half(g, hooks):
        tile = min(256, ff)
        span = slice(g * held, (g + 1) * held)

        def give(i):
            send(part.at[g, i], other.at[g, i], y_send.at[g, i], y_recv.at[g, i], pair)

        for i, matrix in enumerate((w_gate, w_up)):
            if g == 0:
                loads[4 + i].wait()

            @pl.loop(0, ff // tile)
            def _(n):
                cols = pl.ds(pl.multiple_of(n * tile, tile), tile)
                part[g, i, :, cols] = jnp.dot(
                    x_ref[span, :], matrix[:, cols], preferred_element_type=jnp.float32
                ).astype(jnp.bfloat16)

            give(i)
            for hook in hooks[i]:
                hook()
        if g == 0:
            loads[6].wait()

        @pl.loop(0, ff // tile)
        def _(n):
            cols = pl.ds(pl.multiple_of(n * tile, tile), tile)
            part[g, 2, :, cols] = contract_cols(eg_ref[span, :], w_down[cols, :]).astype(
                jnp.bfloat16
            )

        give(2)
        for hook in hooks[2]:
            hook()

    def second_half(g):
        span = slice(g * held, (g + 1) * held)
        for i in range(3):
            arrived(other.at[g, i], y_send.at[g, i], y_recv.at[g, i], pair)
        gate, up_value, hidden_grad = [
            part[g, i].astype(jnp.float32) + other[g, i].astype(jnp.float32) for i in range(3)
        ]
        sig = jax.nn.sigmoid(gate)
        silu = gate * sig
        hidden_ref[span, :] = (silu * up_value).astype(jnp.bfloat16)
        gg_ref[span, :] = (
            hidden_grad * up_value * sig * (1.0 + gate * (1.0 - sig))
        ).astype(jnp.bfloat16)
        ug_ref[span, :] = (hidden_grad * silu).astype(jnp.bfloat16)
        tile = min(512, wide)

        @pl.loop(0, wide // tile)
        def _(n):
            cols = pl.ds(pl.multiple_of(n * tile, tile), tile)
            out = jnp.dot(
                hidden_ref[span, :], w_down[:, cols], preferred_element_type=jnp.float32
            ) * scale[span, 0:1]
            back_in = contract_cols(gg_ref[span, :], w_gate[cols, :]) + contract_cols(
                ug_ref[span, :], w_up[cols, :]
            )
            for p in range(per):
                for s in range(2):
                    for c in range(2):
                        first = p * chunk + (2 * s + c) * rows
                        block = slice(first, first + rows)
                        back[g * per + p, c, s, :, cols] = jnp.concatenate(
                            [out[block], back_in[block]], axis=0
                        ).astype(jnp.bfloat16)

        for k in range(g * per, (g + 1) * per):
            send(back.at[k, 1 - core], back_sib.at[k], r1_send.at[k], r1_recv.at[k], sibling)

    def sum_core(k):
        arrived(back_sib.at[k], r1_send.at[k], r1_recv.at[k], sibling)
        mid[k] = (
            back[k, core].astype(jnp.float32) + back_sib[k].astype(jnp.float32)
        ).astype(jnp.bfloat16)
        send(mid.at[k, 1 - side], mid_x.at[k], r2_send.at[k], r2_recv.at[k], across)

    def sum_side(k):
        arrived(mid_x.at[k], r2_send.at[k], r2_recv.at[k], across)
        last[k] = (
            mid[k, side].astype(jnp.float32) + mid_x[k].astype(jnp.float32)
        ).astype(jnp.bfloat16)
        if k > 0:
            send(last.at[k], last_z.at[k], r3_send.at[k], r3_recv.at[k], in_plane(k))

    own = msg.at[0, side, core]
    spread(0)
    for k in range(1, planes):
        send(own, msg.at[k, side, core], z_send.at[k], z_recv.at[k], in_plane(k))

    for k in range(per):
        relay(k)
        if k + 1 < per:
            spread(k + 1)
    for g in range(groups):
        for k in range(g * per, (g + 1) * per):
            gather_end(k)
            gather_rows(k)
        hooks = [[], [], []]
        if g + 1 < groups:
            coming = range((g + 1) * per, (g + 2) * per)
            hooks[0] = [functools.partial(spread, coming[0])]
            hooks[1] = [functools.partial(spread, k) for k in coming[1:]]
            hooks[1].append(functools.partial(relay, coming[0]))
            hooks[2] = [functools.partial(relay, k) for k in coming[1:]]
        first_half(g, hooks)
    for g in range(groups):
        second_half(g)
        if g > 0:
            for k in range((g - 1) * per, g * per):
                sum_side(k)
        for k in range(g * per, (g + 1) * per):
            sum_core(k)
    for k in range((groups - 1) * per, planes):
        sum_side(k)

    total = last[0].astype(jnp.float32)
    for k in range(1, planes):
        arrived(last_z.at[k], r3_send.at[k], r3_recv.at[k], in_plane(k))
        total = total + last_z[k].astype(jnp.float32)
    sum_ref[...] = total.astype(jnp.bfloat16)
    for copy in sends:
        copy.wait_send()


def exchange(tokens, expert_ids, route_weights, w_gate, w_up, w_down, grad_out):
    rows, wide = tokens.shape
    ff = w_gate.shape[2]
    experts = lax.axis_size("expert")
    planes = experts // 4
    total = experts * rows
    chunk = 4 * rows
    bf16 = jnp.bfloat16
    per = max(1, planes // 2)
    groups = planes // per
    vmem = pl.BlockSpec(memory_space=pltpu.VMEM)
    hbm = pl.BlockSpec(memory_space=pltpu.HBM)
    dma = pltpu.SemaphoreType.DMA
    return pl.pallas_call(
        functools.partial(exchange_kernel, planes, per),
        out_shape=(
            jax.ShapeDtypeStruct((total, wide), bf16),
            jax.ShapeDtypeStruct((total, wide), bf16),
            jax.ShapeDtypeStruct((total, ff), bf16),
            jax.ShapeDtypeStruct((total, ff), bf16),
            jax.ShapeDtypeStruct((total, ff), bf16),
            jax.ShapeDtypeStruct((2 * rows, wide), bf16),
        ),
        in_specs=[hbm] * 7,
        out_specs=(vmem,) * 6,
        scratch_shapes=[
            pltpu.VMEM((rows, wide), bf16),
            pltpu.VMEM((rows, wide), bf16),
            pltpu.VMEM(expert_ids.shape, expert_ids.dtype),
            pltpu.VMEM(route_weights.shape, route_weights.dtype),
            pltpu.VMEM((wide, ff), bf16),
            pltpu.VMEM((wide, ff), bf16),
            pltpu.VMEM((ff, wide), bf16),
            dma((7,)),
            pltpu.VMEM((planes, 2, 2, 2 * rows, wide + 2 * LANES), bf16),
            pltpu.VMEM((total, LANES), jnp.float32),
            pltpu.VMEM((groups, 3, per * chunk, ff), bf16),
            pltpu.VMEM((groups, 3, per * chunk, ff), bf16),
            pltpu.VMEM((planes, 2, 2, 2 * rows, wide), bf16),
            pltpu.VMEM((planes, 2, 2 * rows, wide), bf16),
            pltpu.VMEM((planes, 2, 2 * rows, wide), bf16),
            pltpu.VMEM((planes, 2 * rows, wide), bf16),
            pltpu.VMEM((planes, 2 * rows, wide), bf16),
            pltpu.VMEM((planes, 2 * rows, wide), bf16),
            dma((planes,)), dma((planes,)),
            dma((planes,)), dma((planes,)),
            dma((planes, 2)), dma((planes, 2)),
            dma((groups, 3)), dma((groups, 3)),
            dma((planes,)), dma((planes,)),
            dma((planes,)), dma((planes,)),
            dma((planes,)), dma((planes,)),
        ],
        compiler_params=pltpu.CompilerParams(
            collective_id=0, has_side_effects=True, vmem_limit_bytes=40 * 1024 * 1024
        ),
        name="exchange",
    )(*[
        pltpu.with_memory_space_constraint(operand, pltpu.HBM)
        for operand in (tokens, grad_out, expert_ids, route_weights, w_gate, w_up, w_down)
    ])


def weights_kernel(x_ref, eg_ref, hidden_ref, gg_ref, ug_ref, sum_ref,
                   out_ref, in_ref, gate_ref, up_ref, down_ref):
    rows = out_ref.shape[0]
    gate_ref[0] = contract_rows(x_ref[...], gg_ref[...]).astype(jnp.bfloat16)
    up_ref[0] = contract_rows(x_ref[...], ug_ref[...]).astype(jnp.bfloat16)
    down_ref[0] = contract_rows(hidden_ref[...], eg_ref[...]).astype(jnp.bfloat16)

    @pl.when(pl.program_id(0) == 0)
    def _():
        both = sum_ref[...].astype(jnp.float32)
        out_ref[...] = both[:rows].astype(jnp.bfloat16)
        in_ref[...] = both[rows:].astype(jnp.bfloat16)


def weight_grads(x, eg, hidden, gg, ug, sums):
    total, wide = x.shape
    ff = hidden.shape[1]
    rows = sums.shape[0] // 2
    tile = min(256, wide)
    bf16 = jnp.bfloat16

    def whole(shape):
        return pl.BlockSpec(shape, lambda n: (0,) * len(shape))

    cols = pl.BlockSpec((total, tile), lambda n: (0, n))
    return pl.pallas_call(
        weights_kernel,
        grid=(wide // tile,),
        out_shape=(
            jax.ShapeDtypeStruct((rows, wide), bf16),
            jax.ShapeDtypeStruct((rows, wide), bf16),
            jax.ShapeDtypeStruct((1, wide, ff), bf16),
            jax.ShapeDtypeStruct((1, wide, ff), bf16),
            jax.ShapeDtypeStruct((1, ff, wide), bf16),
        ),
        in_specs=[cols, cols] + [whole((total, ff))] * 3 + [whole((2 * rows, wide))],
        out_specs=(
            whole((rows, wide)),
            whole((rows, wide)),
            pl.BlockSpec((1, tile, ff), lambda n: (0, n, 0)),
            pl.BlockSpec((1, tile, ff), lambda n: (0, n, 0)),
            pl.BlockSpec((1, ff, tile), lambda n: (0, 0, n)),
        ),
        compiler_params=pltpu.CompilerParams(vmem_limit_bytes=32 * 1024 * 1024),
        name="weight_grads",
    )(x, eg, hidden, gg, ug, sums)


def local(tokens, expert_ids, route_weights, w_gate, w_up, w_down, grad_out):
    experts = lax.axis_size("expert")
    planes = experts // 4
    fits = (
        lax.axis_size("dp") == 2
        and experts % 4 == 0
        and planes & (planes - 1) == 0
        and planes <= 4
        and experts <= LANES
        and tokens.shape[0] % 8 == 0
    )
    if not fits:
        return general(tokens, expert_ids, route_weights, w_gate, w_up, w_down, grad_out)
    return weight_grads(
        *exchange(tokens, expert_ids, route_weights, w_gate, w_up, w_down, grad_out)
    )


def solution(mesh):
    return jax.shard_map(
        local,
        mesh=mesh,
        in_specs=(
            P("expert", "dp"),
            P("expert", None),
            P("expert", None),
            P("expert", "dp", None),
            P("expert", "dp", None),
            P("expert", None, "dp"),
            P("expert", "dp"),
        ),
        out_specs=(
            P("expert", "dp"),
            P("expert", "dp"),
            P("expert", "dp", None),
            P("expert", "dp", None),
            P("expert", None, "dp"),
        ),
        check_vma=False,
    )
```

```python
import functools

import jax
import jax.numpy as jnp
from jax import lax
from jax.experimental import pallas as pl
from jax.experimental.pallas import tpu as pltpu
from jax.sharding import PartitionSpec as P

MESH = pl.DeviceIdType.MESH
LANES = 128


def slot_table(id_block, experts, capacity):
    flat_ids = id_block.reshape(-1)
    onehot = (flat_ids[:, None] == jnp.arange(experts, dtype=jnp.int32)[None, :]).astype(jnp.int32)
    before = jnp.cumsum(onehot, axis=0) - onehot
    slot_index = jnp.sum(before * onehot, axis=1)
    target = flat_ids * capacity + slot_index
    row_index = jnp.arange(experts * capacity, dtype=jnp.int32)
    return (row_index[:, None] == target[None, :]).astype(jnp.bfloat16)


def gate_grads(hidden_grad, gate, up_value):
    sigmoid_gate = jax.nn.sigmoid(gate)
    silu_gate = gate * sigmoid_gate
    gate_grad = (
        hidden_grad * up_value * sigmoid_gate * (1.0 + gate * (1.0 - sigmoid_gate))
    ).astype(jnp.bfloat16)
    up_grad = (hidden_grad * silu_gate).astype(jnp.bfloat16)
    return (gate_grad, up_grad)


def contract_rows(left, right):
    return lax.dot_general(
        left, right, (((0,), (0,)), ((), ())), preferred_element_type=jnp.float32
    )


def contract_cols(left, right):
    return lax.dot_general(
        left, right, (((1,), (1,)), ((), ())), preferred_element_type=jnp.float32
    )


def general(tokens, expert_ids, route_weights, w_gate, w_up, w_down, grad_out):
    tok_rows = tokens.shape[0]
    slices = tokens.shape[1]
    top_count = expert_ids.shape[1]
    experts = lax.axis_size("expert")
    capacity = min(tok_rows, 3 * tok_rows * top_count // experts)
    table = slot_table(expert_ids, experts, capacity)
    weight_flat = route_weights.reshape(-1)
    token_replicas = jnp.repeat(tokens, top_count, axis=0)
    grad_rep = (
        jnp.repeat(grad_out, top_count, axis=0).astype(jnp.float32) * weight_flat[:, None]
    ).astype(jnp.bfloat16)
    dispatch_token_rows = jnp.dot(table, token_replicas, preferred_element_type=jnp.float32).astype(
        jnp.bfloat16
    )
    dispatch_gradients = jnp.dot(table, grad_rep, preferred_element_type=jnp.float32).astype(
        jnp.bfloat16
    )
    dispatch_token_rows = dispatch_token_rows.reshape(experts, capacity, slices)
    dispatch_gradients = dispatch_gradients.reshape(experts, capacity, slices)
    expert_in, expert_grad = (
        lax.all_to_all(dispatch_token_rows, "expert", split_axis=0, concat_axis=0, tiled=True),
        lax.all_to_all(dispatch_gradients, "expert", split_axis=0, concat_axis=0, tiled=True),
    )
    expert_in = expert_in.reshape(-1, slices)
    expert_grad = expert_grad.reshape(-1, slices)
    gate_matrix = w_gate[0]
    up_matrix = w_up[0]
    down_matrix = w_down[0]
    gate_part = jnp.dot(expert_in, gate_matrix, preferred_element_type=jnp.float32)
    up_part = jnp.dot(expert_in, up_matrix, preferred_element_type=jnp.float32)
    gate, up_value = (
        lax.psum(gate_part.astype(jnp.bfloat16), "dp").astype(jnp.float32),
        lax.psum(up_part.astype(jnp.bfloat16), "dp").astype(jnp.float32),
    )
    hidden = (gate * jax.nn.sigmoid(gate) * up_value).astype(jnp.bfloat16)
    expert_out = jnp.dot(hidden, down_matrix, preferred_element_type=jnp.float32).astype(
        jnp.bfloat16
    )
    out_blocks = expert_out.reshape(experts, capacity, slices)
    grad_part = contract_cols(expert_grad, down_matrix)
    hidden_grad = lax.psum(grad_part.astype(jnp.bfloat16), "dp").astype(jnp.float32)
    gate_grad, up_grad = gate_grads(hidden_grad, gate, up_value)
    down_grad = contract_rows(hidden, expert_grad).astype(jnp.bfloat16)
    gate_weight = contract_rows(expert_in, gate_grad).astype(jnp.bfloat16)
    up_weight = contract_rows(expert_in, up_grad).astype(jnp.bfloat16)
    input_rows = (contract_cols(gate_grad, gate_matrix) + contract_cols(up_grad, up_matrix)).astype(
        jnp.bfloat16
    )
    input_blocks = input_rows.reshape(experts, capacity, slices)
    out_back, input_back = (
        lax.all_to_all(out_blocks, "expert", split_axis=0, concat_axis=0, tiled=True),
        lax.all_to_all(input_blocks, "expert", split_axis=0, concat_axis=0, tiled=True),
    )
    backward_output = contract_rows(table, out_back.reshape(-1, slices)).reshape(
        tok_rows, top_count, slices
    )
    backward_input = contract_rows(table, input_back.reshape(-1, slices)).reshape(
        tok_rows, top_count, slices
    )
    layer_out = jnp.sum(backward_output * route_weights[:, :, None], axis=1).astype(jnp.bfloat16)
    input_grad = jnp.sum(backward_input, axis=1).astype(jnp.bfloat16)
    return (layer_out, input_grad, gate_weight[None], up_weight[None], down_grad[None])


def partner(index, step):
    bit = 1
    while bit <= step:
        if step & bit:
            index = index + bit - 2 * bit * ((index // bit) % 2)
        bit *= 2
    return index


def exchange_kernel(
    planes, per,
    tok_hbm, grad_hbm, id_hbm, weight_hbm, gate_hbm, up_hbm, down_hbm,
    x_ref, eg_ref, hidden_ref, gg_ref, ug_ref, sum_ref,
    tok_ref, grad_ref, id_ref, weight_ref,
    w_gate, w_up, w_down, load_sem,
    msg, scale, part, other, back, back_sib, mid, mid_x, last, last_z,
    z_send, z_recv, x_send, x_recv, s_send, s_recv, y_send, y_recv,
    r1_send, r1_recv, r2_send, r2_recv, r3_send, r3_recv,
):
    rows, wide = tok_ref.shape
    ff = w_gate.shape[1]
    top = id_ref.shape[1]
    chunk = 4 * rows
    groups = planes // per
    held = per * chunk
    me = lax.axis_index("expert")
    core = me % 2
    side = (me // 2) % 2
    plane = me // 4
    pair = {"dp": 1 - lax.axis_index("dp")}
    sibling = {"expert": plane * 4 + side * 2 + (1 - core)}
    across = {"expert": plane * 4 + (1 - side) * 2 + core}

    def in_plane(step):
        return {"expert": partner(plane, step) * 4 + side * 2 + core}

    loads = []
    for i, (source, target) in enumerate((
        (tok_hbm, tok_ref), (grad_hbm, grad_ref), (id_hbm, id_ref), (weight_hbm, weight_ref),
        (gate_hbm.at[0], w_gate), (up_hbm.at[0], w_up), (down_hbm.at[0], w_down),
    )):
        load = pltpu.make_async_copy(source, target, load_sem.at[i])
        load.start()
        loads.append(load)

    peers = [sibling, across, pair] + [in_plane(step) for step in range(1, planes)]
    barrier = pltpu.get_barrier_semaphore()
    for peer in peers:
        pl.semaphore_signal(barrier, inc=1, device_id=peer, device_id_type=MESH)

    for load in loads[:4]:
        load.wait()
    lane = lax.broadcasted_iota(jnp.int32, (rows, LANES), 1)
    dense = jnp.zeros((rows, LANES), jnp.float32)
    chosen = jnp.zeros((rows, LANES), jnp.float32)
    for k in range(top):
        hit = id_ref[:, k:k + 1] == lane
        dense = dense + jnp.where(hit, weight_ref[:, k:k + 1], 0.0)
        chosen = chosen + jnp.where(hit, 1.0, 0.0)
    high = dense.astype(jnp.bfloat16).astype(jnp.float32)
    middle = (dense - high).astype(jnp.bfloat16).astype(jnp.float32)
    low = dense - high - middle
    both = jnp.concatenate(
        [tok_ref[...].astype(jnp.float32), grad_ref[...].astype(jnp.float32)], axis=0
    )
    extra_a = jnp.concatenate([high, low], axis=0)
    extra_b = jnp.concatenate([middle, chosen], axis=0)
    msg[0, side, core, :, :wide] = both.astype(jnp.bfloat16)
    msg[0, side, core, :, wide:wide + LANES] = extra_a.astype(jnp.bfloat16)
    msg[0, side, core, :, wide + LANES:] = extra_b.astype(jnp.bfloat16)

    pl.semaphore_wait(barrier, len(peers))

    sends = []

    def send(source, target, send_sem, recv_sem, device):
        copy = pltpu.make_async_remote_copy(
            src_ref=source, dst_ref=target, send_sem=send_sem, recv_sem=recv_sem,
            device_id=device, device_id_type=MESH,
        )
        copy.start()
        sends.append(copy)

    def arrived(target, send_sem, recv_sem, device):
        pltpu.make_async_remote_copy(
            src_ref=target, dst_ref=target, send_sem=send_sem, recv_sem=recv_sem,
            device_id=device, device_id_type=MESH,
        ).wait_recv()

    def spread(k):
        own = msg.at[k, side, core]
        if k > 0:
            arrived(own, z_send.at[k], z_recv.at[k], in_plane(k))
        send(own, own, x_send.at[k], x_recv.at[k], across)
        send(own, own, s_send.at[k, 0], s_recv.at[k, 0], sibling)

    def relay(k):
        far = msg.at[k, 1 - side, core]
        arrived(far, x_send.at[k], x_recv.at[k], across)
        send(far, far, s_send.at[k, 1], s_recv.at[k, 1], sibling)

    def gather_end(k):
        arrived(msg.at[k, side, 1 - core], s_send.at[k, 0], s_recv.at[k, 0], sibling)
        arrived(msg.at[k, 1 - side, 1 - core], s_send.at[k, 1], s_recv.at[k, 1], sibling)

    def gather_rows(k):
        mine = lax.broadcasted_iota(jnp.int32, (rows, LANES), 1) == me
        at = k * chunk
        for s in range(2):
            ins, grads = [], []
            for c in range(2):
                extra = msg[k, s, c, :, wide:].astype(jnp.float32)
                dense_w = extra[:rows, :LANES] + extra[:rows, LANES:] + extra[rows:, :LANES]
                weight = jnp.sum(jnp.where(mine, dense_w, 0.0), axis=1, keepdims=True)
                mask = jnp.sum(jnp.where(mine, extra[rows:, LANES:], 0.0), axis=1, keepdims=True)
                body = msg[k, s, c, :, :wide].astype(jnp.float32)
                ins.append(body[:rows] * mask)
                grads.append(body[rows:] * weight)
                first = at + (2 * s + c) * rows
                scale[first:first + rows, :] = jnp.broadcast_to(weight, (rows, LANES))
            here = slice(at + 2 * s * rows, at + 2 * (s + 1) * rows)
            x_ref[here, :] = jnp.concatenate(ins, axis=0).astype(jnp.bfloat16)
            eg_ref[here, :] = jnp.concatenate(grads, axis=0).astype(jnp.bfloat16)

    def first_half(g, hooks):
        tile = min(256, ff)
        span = slice(g * held, (g + 1) * held)

        def give(i):
            send(part.at[g, i], other.at[g, i], y_send.at[g, i], y_recv.at[g, i], pair)

        for i, matrix in enumerate((w_gate, w_up)):
            if g == 0:
                loads[4 + i].wait()

            @pl.loop(0, ff // tile)
            def _(n):
                cols = pl.ds(pl.multiple_of(n * tile, tile), tile)
                part[g, i, :, cols] = jnp.dot(
                    x_ref[span, :], matrix[:, cols], preferred_element_type=jnp.float32
                ).astype(jnp.bfloat16)

            give(i)
            for hook in hooks[i]:
                hook()
        if g == 0:
            loads[6].wait()

        @pl.loop(0, ff // tile)
        def _(n):
            cols = pl.ds(pl.multiple_of(n * tile, tile), tile)
            part[g, 2, :, cols] = contract_cols(eg_ref[span, :], w_down[cols, :]).astype(
                jnp.bfloat16
            )

        give(2)
        for hook in hooks[2]:
            hook()

    def second_half(g):
        span = slice(g * held, (g + 1) * held)
        for i in range(3):
            arrived(other.at[g, i], y_send.at[g, i], y_recv.at[g, i], pair)
        gate, up_value, hidden_grad = [
            part[g, i].astype(jnp.float32) + other[g, i].astype(jnp.float32) for i in range(3)
        ]
        sig = jax.nn.sigmoid(gate)
        silu = gate * sig
        hidden_ref[span, :] = (silu * up_value).astype(jnp.bfloat16)
        gg_ref[span, :] = (
            hidden_grad * up_value * sig * (1.0 + gate * (1.0 - sig))
        ).astype(jnp.bfloat16)
        ug_ref[span, :] = (hidden_grad * silu).astype(jnp.bfloat16)
        tile = min(512, wide)

        @pl.loop(0, wide // tile)
        def _(n):
            cols = pl.ds(pl.multiple_of(n * tile, tile), tile)
            out = jnp.dot(
                hidden_ref[span, :], w_down[:, cols], preferred_element_type=jnp.float32
            ) * scale[span, 0:1]
            back_in = contract_cols(gg_ref[span, :], w_gate[cols, :]) + contract_cols(
                ug_ref[span, :], w_up[cols, :]
            )
            for p in range(per):
                for s in range(2):
                    for c in range(2):
                        first = p * chunk + (2 * s + c) * rows
                        block = slice(first, first + rows)
                        back[g * per + p, c, s, :, cols] = jnp.concatenate(
                            [out[block], back_in[block]], axis=0
                        ).astype(jnp.bfloat16)

        for k in range(g * per, (g + 1) * per):
            send(back.at[k, 1 - core], back_sib.at[k], r1_send.at[k], r1_recv.at[k], sibling)

    def sum_core(k):
        arrived(back_sib.at[k], r1_send.at[k], r1_recv.at[k], sibling)
        mid[k] = (
            back[k, core].astype(jnp.float32) + back_sib[k].astype(jnp.float32)
        ).astype(jnp.bfloat16)
        send(mid.at[k, 1 - side], mid_x.at[k], r2_send.at[k], r2_recv.at[k], across)

    def sum_side(k):
        arrived(mid_x.at[k], r2_send.at[k], r2_recv.at[k], across)
        last[k] = (
            mid[k, side].astype(jnp.float32) + mid_x[k].astype(jnp.float32)
        ).astype(jnp.bfloat16)
        if k > 0:
            send(last.at[k], last_z.at[k], r3_send.at[k], r3_recv.at[k], in_plane(k))

    order = [0] + list(range(2, planes)) + list(range(1, min(2, planes)))
    own = msg.at[0, side, core]
    spread(0)
    for k in order[1:]:
        send(own, msg.at[k, side, core], z_send.at[k], z_recv.at[k], in_plane(k))
    relay(0)
    if planes > 1:
        spread(order[1])

    def begin(i):
        gather_end(order[i])
        gather_rows(order[i])
        hooks = [[], [], []]
        if i + 1 < planes:
            hooks[0] = [functools.partial(relay, order[i + 1])]
        if i + 2 < planes:
            hooks[2] = [functools.partial(spread, order[i + 2])]
        first_half(order[i], hooks)

    ahead = min(3, planes)
    for i in range(ahead):
        begin(i)
    for i in range(planes):
        second_half(order[i])
        if i + ahead < planes:
            begin(i + ahead)
        if i > 0:
            sum_side(order[i - 1])
        sum_core(order[i])
    sum_side(order[-1])

    total = last[0].astype(jnp.float32)
    for k in range(1, planes):
        arrived(last_z.at[k], r3_send.at[k], r3_recv.at[k], in_plane(k))
        total = total + last_z[k].astype(jnp.float32)
    sum_ref[...] = total.astype(jnp.bfloat16)
    for copy in sends:
        copy.wait_send()


def exchange(tokens, expert_ids, route_weights, w_gate, w_up, w_down, grad_out):
    rows, wide = tokens.shape
    ff = w_gate.shape[2]
    experts = lax.axis_size("expert")
    planes = experts // 4
    total = experts * rows
    chunk = 4 * rows
    bf16 = jnp.bfloat16
    per = 1
    groups = planes // per
    vmem = pl.BlockSpec(memory_space=pltpu.VMEM)
    hbm = pl.BlockSpec(memory_space=pltpu.HBM)
    dma = pltpu.SemaphoreType.DMA
    return pl.pallas_call(
        functools.partial(exchange_kernel, planes, per),
        out_shape=(
            jax.ShapeDtypeStruct((total, wide), bf16),
            jax.ShapeDtypeStruct((total, wide), bf16),
            jax.ShapeDtypeStruct((total, ff), bf16),
            jax.ShapeDtypeStruct((total, ff), bf16),
            jax.ShapeDtypeStruct((total, ff), bf16),
            jax.ShapeDtypeStruct((2 * rows, wide), bf16),
        ),
        in_specs=[hbm] * 7,
        out_specs=(vmem,) * 6,
        scratch_shapes=[
            pltpu.VMEM((rows, wide), bf16),
            pltpu.VMEM((rows, wide), bf16),
            pltpu.VMEM(expert_ids.shape, expert_ids.dtype),
            pltpu.VMEM(route_weights.shape, route_weights.dtype),
            pltpu.VMEM((wide, ff), bf16),
            pltpu.VMEM((wide, ff), bf16),
            pltpu.VMEM((ff, wide), bf16),
            dma((7,)),
            pltpu.VMEM((planes, 2, 2, 2 * rows, wide + 2 * LANES), bf16),
            pltpu.VMEM((total, LANES), jnp.float32),
            pltpu.VMEM((groups, 3, per * chunk, ff), bf16),
            pltpu.VMEM((groups, 3, per * chunk, ff), bf16),
            pltpu.VMEM((planes, 2, 2, 2 * rows, wide), bf16),
            pltpu.VMEM((planes, 2, 2 * rows, wide), bf16),
            pltpu.VMEM((planes, 2, 2 * rows, wide), bf16),
            pltpu.VMEM((planes, 2 * rows, wide), bf16),
            pltpu.VMEM((planes, 2 * rows, wide), bf16),
            pltpu.VMEM((planes, 2 * rows, wide), bf16),
            dma((planes,)), dma((planes,)),
            dma((planes,)), dma((planes,)),
            dma((planes, 2)), dma((planes, 2)),
            dma((groups, 3)), dma((groups, 3)),
            dma((planes,)), dma((planes,)),
            dma((planes,)), dma((planes,)),
            dma((planes,)), dma((planes,)),
        ],
        compiler_params=pltpu.CompilerParams(
            collective_id=0, has_side_effects=True, vmem_limit_bytes=40 * 1024 * 1024
        ),
        name="exchange",
    )(*[
        pltpu.with_memory_space_constraint(operand, pltpu.HBM)
        for operand in (tokens, grad_out, expert_ids, route_weights, w_gate, w_up, w_down)
    ])


def weights_kernel(x_ref, eg_ref, hidden_ref, gg_ref, ug_ref, sum_ref,
                   out_ref, in_ref, gate_ref, up_ref, down_ref):
    rows = out_ref.shape[0]
    gate_ref[0] = contract_rows(x_ref[...], gg_ref[...]).astype(jnp.bfloat16)
    up_ref[0] = contract_rows(x_ref[...], ug_ref[...]).astype(jnp.bfloat16)
    down_ref[0] = contract_rows(hidden_ref[...], eg_ref[...]).astype(jnp.bfloat16)

    @pl.when(pl.program_id(0) == 0)
    def _():
        both = sum_ref[...].astype(jnp.float32)
        out_ref[...] = both[:rows].astype(jnp.bfloat16)
        in_ref[...] = both[rows:].astype(jnp.bfloat16)


def weight_grads(x, eg, hidden, gg, ug, sums):
    total, wide = x.shape
    ff = hidden.shape[1]
    rows = sums.shape[0] // 2
    tile = min(256, wide)
    bf16 = jnp.bfloat16

    def whole(shape):
        return pl.BlockSpec(shape, lambda n: (0,) * len(shape))

    cols = pl.BlockSpec((total, tile), lambda n: (0, n))
    return pl.pallas_call(
        weights_kernel,
        grid=(wide // tile,),
        out_shape=(
            jax.ShapeDtypeStruct((rows, wide), bf16),
            jax.ShapeDtypeStruct((rows, wide), bf16),
            jax.ShapeDtypeStruct((1, wide, ff), bf16),
            jax.ShapeDtypeStruct((1, wide, ff), bf16),
            jax.ShapeDtypeStruct((1, ff, wide), bf16),
        ),
        in_specs=[cols, cols] + [whole((total, ff))] * 3 + [whole((2 * rows, wide))],
        out_specs=(
            whole((rows, wide)),
            whole((rows, wide)),
            pl.BlockSpec((1, tile, ff), lambda n: (0, n, 0)),
            pl.BlockSpec((1, tile, ff), lambda n: (0, n, 0)),
            pl.BlockSpec((1, ff, tile), lambda n: (0, 0, n)),
        ),
        compiler_params=pltpu.CompilerParams(vmem_limit_bytes=32 * 1024 * 1024),
        name="weight_grads",
    )(x, eg, hidden, gg, ug, sums)


def local(tokens, expert_ids, route_weights, w_gate, w_up, w_down, grad_out):
    experts = lax.axis_size("expert")
    planes = experts // 4
    fits = (
        lax.axis_size("dp") == 2
        and experts % 4 == 0
        and planes & (planes - 1) == 0
        and planes <= 4
        and experts <= LANES
        and tokens.shape[0] % 8 == 0
    )
    if not fits:
        return general(tokens, expert_ids, route_weights, w_gate, w_up, w_down, grad_out)
    return weight_grads(
        *exchange(tokens, expert_ids, route_weights, w_gate, w_up, w_down, grad_out)
    )


def solution(mesh):
    return jax.shard_map(
        local,
        mesh=mesh,
        in_specs=(
            P("expert", "dp"),
            P("expert", None),
            P("expert", None),
            P("expert", "dp", None),
            P("expert", "dp", None),
            P("expert", None, "dp"),
            P("expert", "dp"),
        ),
        out_specs=(
            P("expert", "dp"),
            P("expert", "dp"),
            P("expert", "dp", None),
            P("expert", "dp", None),
            P("expert", None, "dp"),
        ),
        check_vma=False,
    )
```

```python
import functools

import jax
import jax.numpy as jnp
from jax import lax
from jax.experimental import pallas as pl
from jax.experimental.pallas import tpu as pltpu
from jax.sharding import PartitionSpec as P

MESH = pl.DeviceIdType.MESH
LANES = 128


def slot_table(id_block, experts, capacity):
    flat_ids = id_block.reshape(-1)
    onehot = (flat_ids[:, None] == jnp.arange(experts, dtype=jnp.int32)[None, :]).astype(jnp.int32)
    before = jnp.cumsum(onehot, axis=0) - onehot
    slot_index = jnp.sum(before * onehot, axis=1)
    target = flat_ids * capacity + slot_index
    row_index = jnp.arange(experts * capacity, dtype=jnp.int32)
    return (row_index[:, None] == target[None, :]).astype(jnp.bfloat16)


def gate_grads(hidden_grad, gate, up_value):
    sigmoid_gate = jax.nn.sigmoid(gate)
    silu_gate = gate * sigmoid_gate
    gate_grad = (
        hidden_grad * up_value * sigmoid_gate * (1.0 + gate * (1.0 - sigmoid_gate))
    ).astype(jnp.bfloat16)
    up_grad = (hidden_grad * silu_gate).astype(jnp.bfloat16)
    return (gate_grad, up_grad)


def contract_rows(left, right):
    return lax.dot_general(
        left, right, (((0,), (0,)), ((), ())), preferred_element_type=jnp.float32
    )


def contract_cols(left, right):
    return lax.dot_general(
        left, right, (((1,), (1,)), ((), ())), preferred_element_type=jnp.float32
    )


def general(tokens, expert_ids, route_weights, w_gate, w_up, w_down, grad_out):
    tok_rows = tokens.shape[0]
    slices = tokens.shape[1]
    top_count = expert_ids.shape[1]
    experts = lax.axis_size("expert")
    capacity = min(tok_rows, 3 * tok_rows * top_count // experts)
    table = slot_table(expert_ids, experts, capacity)
    weight_flat = route_weights.reshape(-1)
    token_replicas = jnp.repeat(tokens, top_count, axis=0)
    grad_rep = (
        jnp.repeat(grad_out, top_count, axis=0).astype(jnp.float32) * weight_flat[:, None]
    ).astype(jnp.bfloat16)
    dispatch_token_rows = jnp.dot(table, token_replicas, preferred_element_type=jnp.float32).astype(
        jnp.bfloat16
    )
    dispatch_gradients = jnp.dot(table, grad_rep, preferred_element_type=jnp.float32).astype(
        jnp.bfloat16
    )
    dispatch_token_rows = dispatch_token_rows.reshape(experts, capacity, slices)
    dispatch_gradients = dispatch_gradients.reshape(experts, capacity, slices)
    expert_in, expert_grad = (
        lax.all_to_all(dispatch_token_rows, "expert", split_axis=0, concat_axis=0, tiled=True),
        lax.all_to_all(dispatch_gradients, "expert", split_axis=0, concat_axis=0, tiled=True),
    )
    expert_in = expert_in.reshape(-1, slices)
    expert_grad = expert_grad.reshape(-1, slices)
    gate_matrix = w_gate[0]
    up_matrix = w_up[0]
    down_matrix = w_down[0]
    gate_part = jnp.dot(expert_in, gate_matrix, preferred_element_type=jnp.float32)
    up_part = jnp.dot(expert_in, up_matrix, preferred_element_type=jnp.float32)
    gate, up_value = (
        lax.psum(gate_part.astype(jnp.bfloat16), "dp").astype(jnp.float32),
        lax.psum(up_part.astype(jnp.bfloat16), "dp").astype(jnp.float32),
    )
    hidden = (gate * jax.nn.sigmoid(gate) * up_value).astype(jnp.bfloat16)
    expert_out = jnp.dot(hidden, down_matrix, preferred_element_type=jnp.float32).astype(
        jnp.bfloat16
    )
    out_blocks = expert_out.reshape(experts, capacity, slices)
    grad_part = contract_cols(expert_grad, down_matrix)
    hidden_grad = lax.psum(grad_part.astype(jnp.bfloat16), "dp").astype(jnp.float32)
    gate_grad, up_grad = gate_grads(hidden_grad, gate, up_value)
    down_grad = contract_rows(hidden, expert_grad).astype(jnp.bfloat16)
    gate_weight = contract_rows(expert_in, gate_grad).astype(jnp.bfloat16)
    up_weight = contract_rows(expert_in, up_grad).astype(jnp.bfloat16)
    input_rows = (contract_cols(gate_grad, gate_matrix) + contract_cols(up_grad, up_matrix)).astype(
        jnp.bfloat16
    )
    input_blocks = input_rows.reshape(experts, capacity, slices)
    out_back, input_back = (
        lax.all_to_all(out_blocks, "expert", split_axis=0, concat_axis=0, tiled=True),
        lax.all_to_all(input_blocks, "expert", split_axis=0, concat_axis=0, tiled=True),
    )
    backward_output = contract_rows(table, out_back.reshape(-1, slices)).reshape(
        tok_rows, top_count, slices
    )
    backward_input = contract_rows(table, input_back.reshape(-1, slices)).reshape(
        tok_rows, top_count, slices
    )
    layer_out = jnp.sum(backward_output * route_weights[:, :, None], axis=1).astype(jnp.bfloat16)
    input_grad = jnp.sum(backward_input, axis=1).astype(jnp.bfloat16)
    return (layer_out, input_grad, gate_weight[None], up_weight[None], down_grad[None])


def partner(index, step):
    bit = 1
    while bit <= step:
        if step & bit:
            index = index + bit - 2 * bit * ((index // bit) % 2)
        bit *= 2
    return index


def exchange_kernel(
    planes, per,
    tok_hbm, grad_hbm, id_hbm, weight_hbm, gate_hbm, up_hbm, down_hbm,
    x_ref, eg_ref, hidden_ref, gg_ref, ug_ref, sum_ref,
    tok_ref, grad_ref, id_ref, weight_ref,
    w_gate, w_up, w_down, load_sem,
    msg, scale, part, other, back, back_sib, mid, mid_x, last, last_z,
    z_send, z_recv, x_send, x_recv, s_send, s_recv, y_send, y_recv,
    r1_send, r1_recv, r2_send, r2_recv, r3_send, r3_recv,
):
    rows, wide = tok_ref.shape
    ff = w_gate.shape[1]
    top = id_ref.shape[1]
    chunk = 4 * rows
    groups = planes // per
    held = per * chunk
    me = lax.axis_index("expert")
    core = me % 2
    side = (me // 2) % 2
    plane = me // 4
    pair = {"dp": 1 - lax.axis_index("dp")}
    sibling = {"expert": plane * 4 + side * 2 + (1 - core)}
    across = {"expert": plane * 4 + (1 - side) * 2 + core}

    def in_plane(step):
        return {"expert": partner(plane, step) * 4 + side * 2 + core}

    loads = []
    for i, (source, target) in enumerate((
        (tok_hbm, tok_ref), (grad_hbm, grad_ref), (id_hbm, id_ref), (weight_hbm, weight_ref),
        (gate_hbm.at[0], w_gate), (up_hbm.at[0], w_up), (down_hbm.at[0], w_down),
    )):
        load = pltpu.make_async_copy(source, target, load_sem.at[i])
        load.start()
        loads.append(load)

    peers = [sibling, across, pair] + [in_plane(step) for step in range(1, planes)]
    barrier = pltpu.get_barrier_semaphore()
    for peer in peers:
        pl.semaphore_signal(barrier, inc=1, device_id=peer, device_id_type=MESH)

    for load in loads[:4]:
        load.wait()
    lane = lax.broadcasted_iota(jnp.int32, (rows, LANES), 1)
    dense = jnp.zeros((rows, LANES), jnp.float32)
    chosen = jnp.zeros((rows, LANES), jnp.float32)
    for k in range(top):
        hit = id_ref[:, k:k + 1] == lane
        dense = dense + jnp.where(hit, weight_ref[:, k:k + 1], 0.0)
        chosen = chosen + jnp.where(hit, 1.0, 0.0)
    high = dense.astype(jnp.bfloat16).astype(jnp.float32)
    middle = (dense - high).astype(jnp.bfloat16).astype(jnp.float32)
    low = dense - high - middle
    both = jnp.concatenate(
        [tok_ref[...].astype(jnp.float32), grad_ref[...].astype(jnp.float32)], axis=0
    )
    extra_a = jnp.concatenate([high, low], axis=0)
    extra_b = jnp.concatenate([middle, chosen], axis=0)
    msg[0, side, core, :, :wide] = both.astype(jnp.bfloat16)
    msg[0, side, core, :, wide:wide + LANES] = extra_a.astype(jnp.bfloat16)
    msg[0, side, core, :, wide + LANES:] = extra_b.astype(jnp.bfloat16)

    pl.semaphore_wait(barrier, len(peers))

    sends = []

    def send(source, target, send_sem, recv_sem, device):
        copy = pltpu.make_async_remote_copy(
            src_ref=source, dst_ref=target, send_sem=send_sem, recv_sem=recv_sem,
            device_id=device, device_id_type=MESH,
        )
        copy.start()
        sends.append(copy)

    def arrived(target, send_sem, recv_sem, device):
        pltpu.make_async_remote_copy(
            src_ref=target, dst_ref=target, send_sem=send_sem, recv_sem=recv_sem,
            device_id=device, device_id_type=MESH,
        ).wait_recv()

    def spread(k):
        own = msg.at[k, side, core]
        if k > 0:
            arrived(own, z_send.at[k], z_recv.at[k], in_plane(k))
        send(own, own, x_send.at[k], x_recv.at[k], across)
        send(own, own, s_send.at[k, 0], s_recv.at[k, 0], sibling)

    def relay(k):
        far = msg.at[k, 1 - side, core]
        arrived(far, x_send.at[k], x_recv.at[k], across)
        send(far, far, s_send.at[k, 1], s_recv.at[k, 1], sibling)

    def gather_end(k):
        arrived(msg.at[k, side, 1 - core], s_send.at[k, 0], s_recv.at[k, 0], sibling)
        arrived(msg.at[k, 1 - side, 1 - core], s_send.at[k, 1], s_recv.at[k, 1], sibling)

    def gather_rows(k):
        mine = lax.broadcasted_iota(jnp.int32, (rows, LANES), 1) == me
        at = k * chunk
        for s in range(2):
            ins, grads = [], []
            for c in range(2):
                extra = msg[k, s, c, :, wide:].astype(jnp.float32)
                dense_w = extra[:rows, :LANES] + extra[:rows, LANES:] + extra[rows:, :LANES]
                weight = jnp.sum(jnp.where(mine, dense_w, 0.0), axis=1, keepdims=True)
                mask = jnp.sum(jnp.where(mine, extra[rows:, LANES:], 0.0), axis=1, keepdims=True)
                body = msg[k, s, c, :, :wide].astype(jnp.float32)
                ins.append(body[:rows] * mask)
                grads.append(body[rows:] * weight)
                first = at + (2 * s + c) * rows
                scale[first:first + rows, :] = jnp.broadcast_to(weight, (rows, LANES))
            here = slice(at + 2 * s * rows, at + 2 * (s + 1) * rows)
            x_ref[here, :] = jnp.concatenate(ins, axis=0).astype(jnp.bfloat16)
            eg_ref[here, :] = jnp.concatenate(grads, axis=0).astype(jnp.bfloat16)

    def first_half(g, hooks):
        tile = ff
        span = slice(g * held, (g + 1) * held)

        def give(i):
            send(part.at[g, i], other.at[g, i], y_send.at[g, i], y_recv.at[g, i], pair)

        for i, matrix in enumerate((w_gate, w_up)):
            if g == 0:
                loads[4 + i].wait()

            @pl.loop(0, ff // tile)
            def _(n):
                cols = pl.ds(pl.multiple_of(n * tile, tile), tile)
                part[g, i, :, cols] = jnp.dot(
                    x_ref[span, :], matrix[:, cols], preferred_element_type=jnp.float32
                ).astype(jnp.bfloat16)

            give(i)
            for hook in hooks[i]:
                hook()
        if g == 0:
            loads[6].wait()

        @pl.loop(0, ff // tile)
        def _(n):
            cols = pl.ds(pl.multiple_of(n * tile, tile), tile)
            part[g, 2, :, cols] = contract_cols(eg_ref[span, :], w_down[cols, :]).astype(
                jnp.bfloat16
            )

        give(2)
        for hook in hooks[2]:
            hook()

    half = wide // 2
    tile_out = min(512, half)

    def give_back(kind, g, product):
        @pl.loop(0, half // tile_out)
        def _(n):
            cols = pl.ds(pl.multiple_of(n * tile_out, tile_out), tile_out)
            high = pl.ds(pl.multiple_of(half + n * tile_out, tile_out), tile_out)
            left, right = product(cols), product(high)
            for p in range(per):
                for s in range(2):
                    for c in range(2):
                        first = p * chunk + (2 * s + c) * rows
                        block = slice(first, first + rows)
                        back[kind, g, c, s, p, :, cols] = jnp.concatenate(
                            [left[block], right[block]], axis=0
                        ).astype(jnp.bfloat16)

        send(
            back.at[kind, g, 1 - core], back_sib.at[kind, g],
            r1_send.at[kind, g], r1_recv.at[kind, g], sibling,
        )

    def summed(g, i):
        arrived(other.at[g, i], y_send.at[g, i], y_recv.at[g, i], pair)
        return part[g, i].astype(jnp.float32) + other[g, i].astype(jnp.float32)

    def outputs(g):
        span = slice(g * held, (g + 1) * held)
        gate, up_value = summed(g, 0), summed(g, 1)
        hidden_ref[span, :] = (gate * jax.nn.sigmoid(gate) * up_value).astype(jnp.bfloat16)
        give_back(0, g, lambda cols: jnp.dot(
            hidden_ref[span, :], w_down[:, cols], preferred_element_type=jnp.float32
        ) * scale[span, 0:1])

    def inputs(g):
        span = slice(g * held, (g + 1) * held)
        hidden_grad = summed(g, 2)
        gate, up_value = [
            part[g, i].astype(jnp.float32) + other[g, i].astype(jnp.float32) for i in range(2)
        ]
        gg_ref[span, :], ug_ref[span, :] = gate_grads(hidden_grad, gate, up_value)
        give_back(1, g, lambda cols: contract_cols(gg_ref[span, :], w_gate[cols, :])
                  + contract_cols(ug_ref[span, :], w_up[cols, :]))

    def sum_core(kind, g):
        arrived(back_sib.at[kind, g], r1_send.at[kind, g], r1_recv.at[kind, g], sibling)
        mid[kind, g] = (
            back[kind, g, core].astype(jnp.float32) + back_sib[kind, g].astype(jnp.float32)
        ).astype(jnp.bfloat16)
        send(
            mid.at[kind, g, 1 - side], mid_x.at[kind, g],
            r2_send.at[kind, g], r2_recv.at[kind, g], across,
        )

    def sum_side(kind, g):
        arrived(mid_x.at[kind, g], r2_send.at[kind, g], r2_recv.at[kind, g], across)
        last[kind, g] = (
            mid[kind, g, side].astype(jnp.float32) + mid_x[kind, g].astype(jnp.float32)
        ).astype(jnp.bfloat16)
        for p in range(per):
            k = g * per + p
            if k > 0:
                send(
                    last.at[kind, g, p], last_z.at[kind, k],
                    r3_send.at[kind, k], r3_recv.at[kind, k], in_plane(k),
                )

    def finish(kind):
        total = last[kind, 0, 0].astype(jnp.float32)
        for k in range(1, planes):
            arrived(last_z.at[kind, k], r3_send.at[kind, k], r3_recv.at[kind, k], in_plane(k))
            total = total + last_z[kind, k].astype(jnp.float32)
        sum_ref[kind] = total.astype(jnp.bfloat16)

    own = msg.at[0, side, core]
    spread(0)
    for k in range(1, planes):
        send(own, msg.at[k, side, core], z_send.at[k], z_recv.at[k], in_plane(k))

    for k in range(per):
        relay(k)
        if k + 1 < per:
            spread(k + 1)
    for g in range(groups):
        for k in range(g * per, (g + 1) * per):
            gather_end(k)
            gather_rows(k)
        hooks = [[], [], []]
        if g + 1 < groups:
            coming = range((g + 1) * per, (g + 2) * per)
            hooks[0] = [functools.partial(spread, coming[0])]
            hooks[1] = [functools.partial(spread, k) for k in coming[1:]]
            hooks[1].append(functools.partial(relay, coming[0]))
            hooks[2] = [functools.partial(relay, k) for k in coming[1:]]
        first_half(g, hooks)
    for g in range(groups):
        outputs(g)
        if g > 0:
            sum_core(1, g - 1)
            sum_side(0, g - 1)
        inputs(g)
        if g > 0:
            sum_side(1, g - 1)
        sum_core(0, g)
    sum_side(0, groups - 1)
    sum_core(1, groups - 1)
    sum_side(1, groups - 1)
    finish(0)
    finish(1)
    for copy in sends:
        copy.wait_send()


def exchange(tokens, expert_ids, route_weights, w_gate, w_up, w_down, grad_out):
    rows, wide = tokens.shape
    ff = w_gate.shape[2]
    experts = lax.axis_size("expert")
    planes = experts // 4
    total = experts * rows
    chunk = 4 * rows
    bf16 = jnp.bfloat16
    per = max(1, planes // 2)
    groups = planes // per
    vmem = pl.BlockSpec(memory_space=pltpu.VMEM)
    hbm = pl.BlockSpec(memory_space=pltpu.HBM)
    dma = pltpu.SemaphoreType.DMA
    return pl.pallas_call(
        functools.partial(exchange_kernel, planes, per),
        out_shape=(
            jax.ShapeDtypeStruct((total, wide), bf16),
            jax.ShapeDtypeStruct((total, wide), bf16),
            jax.ShapeDtypeStruct((total, ff), bf16),
            jax.ShapeDtypeStruct((total, ff), bf16),
            jax.ShapeDtypeStruct((total, ff), bf16),
            jax.ShapeDtypeStruct((2, 2 * rows, wide // 2), bf16),
        ),
        in_specs=[hbm] * 7,
        out_specs=(vmem,) * 6,
        scratch_shapes=[
            pltpu.VMEM((rows, wide), bf16),
            pltpu.VMEM((rows, wide), bf16),
            pltpu.VMEM(expert_ids.shape, expert_ids.dtype),
            pltpu.VMEM(route_weights.shape, route_weights.dtype),
            pltpu.VMEM((wide, ff), bf16),
            pltpu.VMEM((wide, ff), bf16),
            pltpu.VMEM((ff, wide), bf16),
            dma((7,)),
            pltpu.VMEM((planes, 2, 2, 2 * rows, wide + 2 * LANES), bf16),
            pltpu.VMEM((total, LANES), jnp.float32),
            pltpu.VMEM((groups, 3, per * chunk, ff), bf16),
            pltpu.VMEM((groups, 3, per * chunk, ff), bf16),
            pltpu.VMEM((2, groups, 2, 2, per, 2 * rows, wide // 2), bf16),
            pltpu.VMEM((2, groups, 2, per, 2 * rows, wide // 2), bf16),
            pltpu.VMEM((2, groups, 2, per, 2 * rows, wide // 2), bf16),
            pltpu.VMEM((2, groups, per, 2 * rows, wide // 2), bf16),
            pltpu.VMEM((2, groups, per, 2 * rows, wide // 2), bf16),
            pltpu.VMEM((2, planes, 2 * rows, wide // 2), bf16),
            dma((planes,)), dma((planes,)),
            dma((planes,)), dma((planes,)),
            dma((planes, 2)), dma((planes, 2)),
            dma((groups, 3)), dma((groups, 3)),
            dma((2, groups)), dma((2, groups)),
            dma((2, groups)), dma((2, groups)),
            dma((2, planes)), dma((2, planes)),
        ],
        compiler_params=pltpu.CompilerParams(
            collective_id=0, has_side_effects=True, vmem_limit_bytes=40 * 1024 * 1024
        ),
        name="exchange",
    )(*[
        pltpu.with_memory_space_constraint(operand, pltpu.HBM)
        for operand in (tokens, grad_out, expert_ids, route_weights, w_gate, w_up, w_down)
    ])


def weights_kernel(x_ref, eg_ref, hidden_ref, gg_ref, ug_ref, sum_ref,
                   out_ref, in_ref, gate_ref, up_ref, down_ref):
    rows = out_ref.shape[0]
    gate_ref[0] = contract_rows(x_ref[...], gg_ref[...]).astype(jnp.bfloat16)
    up_ref[0] = contract_rows(x_ref[...], ug_ref[...]).astype(jnp.bfloat16)
    down_ref[0] = contract_rows(hidden_ref[...], eg_ref[...]).astype(jnp.bfloat16)

    @pl.when(pl.program_id(0) == 0)
    def _():
        for kind, ref in enumerate((out_ref, in_ref)):
            both = sum_ref[kind].astype(jnp.float32)
            half = both.shape[1]
            ref[:, :half] = both[:rows].astype(jnp.bfloat16)
            ref[:, half:] = both[rows:].astype(jnp.bfloat16)


def weight_grads(x, eg, hidden, gg, ug, sums):
    total, wide = x.shape
    ff = hidden.shape[1]
    rows = sums.shape[1] // 2
    tile = min(256, wide)
    bf16 = jnp.bfloat16

    def whole(shape):
        return pl.BlockSpec(shape, lambda n: (0,) * len(shape))

    cols = pl.BlockSpec((total, tile), lambda n: (0, n))
    return pl.pallas_call(
        weights_kernel,
        grid=(wide // tile,),
        out_shape=(
            jax.ShapeDtypeStruct((rows, wide), bf16),
            jax.ShapeDtypeStruct((rows, wide), bf16),
            jax.ShapeDtypeStruct((1, wide, ff), bf16),
            jax.ShapeDtypeStruct((1, wide, ff), bf16),
            jax.ShapeDtypeStruct((1, ff, wide), bf16),
        ),
        in_specs=[cols, cols] + [whole((total, ff))] * 3 + [whole((2, 2 * rows, wide // 2))],
        out_specs=(
            whole((rows, wide)),
            whole((rows, wide)),
            pl.BlockSpec((1, tile, ff), lambda n: (0, n, 0)),
            pl.BlockSpec((1, tile, ff), lambda n: (0, n, 0)),
            pl.BlockSpec((1, ff, tile), lambda n: (0, 0, n)),
        ),
        compiler_params=pltpu.CompilerParams(vmem_limit_bytes=32 * 1024 * 1024),
        name="weight_grads",
    )(x, eg, hidden, gg, ug, sums)


def local(tokens, expert_ids, route_weights, w_gate, w_up, w_down, grad_out):
    experts = lax.axis_size("expert")
    planes = experts // 4
    fits = (
        lax.axis_size("dp") == 2
        and experts % 4 == 0
        and planes & (planes - 1) == 0
        and planes <= 4
        and experts <= LANES
        and tokens.shape[0] % 8 == 0
    )
    if not fits:
        return general(tokens, expert_ids, route_weights, w_gate, w_up, w_down, grad_out)
    return weight_grads(
        *exchange(tokens, expert_ids, route_weights, w_gate, w_up, w_down, grad_out)
    )


def solution(mesh):
    return jax.shard_map(
        local,
        mesh=mesh,
        in_specs=(
            P("expert", "dp"),
            P("expert", None),
            P("expert", None),
            P("expert", "dp", None),
            P("expert", "dp", None),
            P("expert", None, "dp"),
            P("expert", "dp"),
        ),
        out_specs=(
            P("expert", "dp"),
            P("expert", "dp"),
            P("expert", "dp", None),
            P("expert", "dp", None),
            P("expert", None, "dp"),
        ),
        check_vma=False,
    )
```

```python
import functools

import jax
import jax.numpy as jnp
from jax import lax
from jax.experimental import pallas as pl
from jax.experimental.pallas import tpu as pltpu
from jax.sharding import PartitionSpec as P

MESH = pl.DeviceIdType.MESH
LANES = 128


def slot_table(id_block, experts, capacity):
    flat_ids = id_block.reshape(-1)
    onehot = (flat_ids[:, None] == jnp.arange(experts, dtype=jnp.int32)[None, :]).astype(jnp.int32)
    before = jnp.cumsum(onehot, axis=0) - onehot
    slot_index = jnp.sum(before * onehot, axis=1)
    target = flat_ids * capacity + slot_index
    row_index = jnp.arange(experts * capacity, dtype=jnp.int32)
    return (row_index[:, None] == target[None, :]).astype(jnp.bfloat16)


def gate_grads(hidden_grad, gate, up_value):
    sigmoid_gate = jax.nn.sigmoid(gate)
    silu_gate = gate * sigmoid_gate
    gate_grad = (
        hidden_grad * up_value * sigmoid_gate * (1.0 + gate * (1.0 - sigmoid_gate))
    ).astype(jnp.bfloat16)
    up_grad = (hidden_grad * silu_gate).astype(jnp.bfloat16)
    return (gate_grad, up_grad)


def contract_rows(left, right):
    return lax.dot_general(
        left, right, (((0,), (0,)), ((), ())), preferred_element_type=jnp.float32
    )


def contract_cols(left, right):
    return lax.dot_general(
        left, right, (((1,), (1,)), ((), ())), preferred_element_type=jnp.float32
    )


def general(tokens, expert_ids, route_weights, w_gate, w_up, w_down, grad_out):
    tok_rows = tokens.shape[0]
    slices = tokens.shape[1]
    top_count = expert_ids.shape[1]
    experts = lax.axis_size("expert")
    capacity = min(tok_rows, 3 * tok_rows * top_count // experts)
    table = slot_table(expert_ids, experts, capacity)
    weight_flat = route_weights.reshape(-1)
    token_replicas = jnp.repeat(tokens, top_count, axis=0)
    grad_rep = (
        jnp.repeat(grad_out, top_count, axis=0).astype(jnp.float32) * weight_flat[:, None]
    ).astype(jnp.bfloat16)
    dispatch_token_rows = jnp.dot(table, token_replicas, preferred_element_type=jnp.float32).astype(
        jnp.bfloat16
    )
    dispatch_gradients = jnp.dot(table, grad_rep, preferred_element_type=jnp.float32).astype(
        jnp.bfloat16
    )
    dispatch_token_rows = dispatch_token_rows.reshape(experts, capacity, slices)
    dispatch_gradients = dispatch_gradients.reshape(experts, capacity, slices)
    expert_in, expert_grad = (
        lax.all_to_all(dispatch_token_rows, "expert", split_axis=0, concat_axis=0, tiled=True),
        lax.all_to_all(dispatch_gradients, "expert", split_axis=0, concat_axis=0, tiled=True),
    )
    expert_in = expert_in.reshape(-1, slices)
    expert_grad = expert_grad.reshape(-1, slices)
    gate_matrix = w_gate[0]
    up_matrix = w_up[0]
    down_matrix = w_down[0]
    gate_part = jnp.dot(expert_in, gate_matrix, preferred_element_type=jnp.float32)
    up_part = jnp.dot(expert_in, up_matrix, preferred_element_type=jnp.float32)
    gate, up_value = (
        lax.psum(gate_part.astype(jnp.bfloat16), "dp").astype(jnp.float32),
        lax.psum(up_part.astype(jnp.bfloat16), "dp").astype(jnp.float32),
    )
    hidden = (gate * jax.nn.sigmoid(gate) * up_value).astype(jnp.bfloat16)
    expert_out = jnp.dot(hidden, down_matrix, preferred_element_type=jnp.float32).astype(
        jnp.bfloat16
    )
    out_blocks = expert_out.reshape(experts, capacity, slices)
    grad_part = contract_cols(expert_grad, down_matrix)
    hidden_grad = lax.psum(grad_part.astype(jnp.bfloat16), "dp").astype(jnp.float32)
    gate_grad, up_grad = gate_grads(hidden_grad, gate, up_value)
    down_grad = contract_rows(hidden, expert_grad).astype(jnp.bfloat16)
    gate_weight = contract_rows(expert_in, gate_grad).astype(jnp.bfloat16)
    up_weight = contract_rows(expert_in, up_grad).astype(jnp.bfloat16)
    input_rows = (contract_cols(gate_grad, gate_matrix) + contract_cols(up_grad, up_matrix)).astype(
        jnp.bfloat16
    )
    input_blocks = input_rows.reshape(experts, capacity, slices)
    out_back, input_back = (
        lax.all_to_all(out_blocks, "expert", split_axis=0, concat_axis=0, tiled=True),
        lax.all_to_all(input_blocks, "expert", split_axis=0, concat_axis=0, tiled=True),
    )
    backward_output = contract_rows(table, out_back.reshape(-1, slices)).reshape(
        tok_rows, top_count, slices
    )
    backward_input = contract_rows(table, input_back.reshape(-1, slices)).reshape(
        tok_rows, top_count, slices
    )
    layer_out = jnp.sum(backward_output * route_weights[:, :, None], axis=1).astype(jnp.bfloat16)
    input_grad = jnp.sum(backward_input, axis=1).astype(jnp.bfloat16)
    return (layer_out, input_grad, gate_weight[None], up_weight[None], down_grad[None])


def partner(index, step):
    bit = 1
    while bit <= step:
        if step & bit:
            index = index + bit - 2 * bit * ((index // bit) % 2)
        bit *= 2
    return index


def exchange_kernel(
    planes, per,
    tok_hbm, grad_hbm, id_hbm, weight_hbm, gate_hbm, up_hbm, down_hbm,
    sum_ref, gate_ref, up_ref, down_ref,
    x_ref, eg_ref, hidden_ref, gg_ref, ug_ref,
    tok_ref, grad_ref, id_ref, weight_ref,
    w_gate, w_up, w_down, load_sem,
    msg, scale, part, other, back, back_sib, mid, mid_x, last, last_z,
    z_send, z_recv, x_send, x_recv, s_send, s_recv, y_send, y_recv,
    r1_send, r1_recv, r2_send, r2_recv, r3_send, r3_recv,
):
    rows, wide = tok_ref.shape
    ff = w_gate.shape[1]
    top = id_ref.shape[1]
    chunk = 4 * rows
    groups = planes // per
    held = per * chunk
    me = lax.axis_index("expert")
    core = me % 2
    side = (me // 2) % 2
    plane = me // 4
    pair = {"dp": 1 - lax.axis_index("dp")}
    sibling = {"expert": plane * 4 + side * 2 + (1 - core)}
    across = {"expert": plane * 4 + (1 - side) * 2 + core}

    def in_plane(step):
        return {"expert": partner(plane, step) * 4 + side * 2 + core}

    loads = []
    for i, (source, target) in enumerate((
        (tok_hbm, tok_ref), (grad_hbm, grad_ref), (id_hbm, id_ref), (weight_hbm, weight_ref),
        (gate_hbm.at[0], w_gate), (up_hbm.at[0], w_up), (down_hbm.at[0], w_down),
    )):
        load = pltpu.make_async_copy(source, target, load_sem.at[i])
        load.start()
        loads.append(load)

    peers = [sibling, across, pair] + [in_plane(step) for step in range(1, planes)]
    barrier = pltpu.get_barrier_semaphore()
    for peer in peers:
        pl.semaphore_signal(barrier, inc=1, device_id=peer, device_id_type=MESH)

    for load in loads[:4]:
        load.wait()
    lane = lax.broadcasted_iota(jnp.int32, (rows, LANES), 1)
    dense = jnp.zeros((rows, LANES), jnp.float32)
    chosen = jnp.zeros((rows, LANES), jnp.float32)
    for k in range(top):
        hit = id_ref[:, k:k + 1] == lane
        dense = dense + jnp.where(hit, weight_ref[:, k:k + 1], 0.0)
        chosen = chosen + jnp.where(hit, 1.0, 0.0)
    high = dense.astype(jnp.bfloat16).astype(jnp.float32)
    middle = (dense - high).astype(jnp.bfloat16).astype(jnp.float32)
    low = dense - high - middle
    both = jnp.concatenate(
        [tok_ref[...].astype(jnp.float32), grad_ref[...].astype(jnp.float32)], axis=0
    )
    extra_a = jnp.concatenate([high, low], axis=0)
    extra_b = jnp.concatenate([middle, chosen], axis=0)
    msg[0, side, core, :, :wide] = both.astype(jnp.bfloat16)
    msg[0, side, core, :, wide:wide + LANES] = extra_a.astype(jnp.bfloat16)
    msg[0, side, core, :, wide + LANES:] = extra_b.astype(jnp.bfloat16)

    pl.semaphore_wait(barrier, len(peers))

    sends = []

    def send(source, target, send_sem, recv_sem, device):
        copy = pltpu.make_async_remote_copy(
            src_ref=source, dst_ref=target, send_sem=send_sem, recv_sem=recv_sem,
            device_id=device, device_id_type=MESH,
        )
        copy.start()
        sends.append(copy)

    def arrived(target, send_sem, recv_sem, device):
        pltpu.make_async_remote_copy(
            src_ref=target, dst_ref=target, send_sem=send_sem, recv_sem=recv_sem,
            device_id=device, device_id_type=MESH,
        ).wait_recv()

    def spread(k):
        own = msg.at[k, side, core]
        if k > 0:
            arrived(own, z_send.at[k], z_recv.at[k], in_plane(k))
        send(own, own, x_send.at[k], x_recv.at[k], across)
        send(own, own, s_send.at[k, 0], s_recv.at[k, 0], sibling)

    def relay(k):
        far = msg.at[k, 1 - side, core]
        arrived(far, x_send.at[k], x_recv.at[k], across)
        send(far, far, s_send.at[k, 1], s_recv.at[k, 1], sibling)

    def gather_end(k):
        arrived(msg.at[k, side, 1 - core], s_send.at[k, 0], s_recv.at[k, 0], sibling)
        arrived(msg.at[k, 1 - side, 1 - core], s_send.at[k, 1], s_recv.at[k, 1], sibling)

    def gather_rows(k):
        mine = lax.broadcasted_iota(jnp.int32, (rows, LANES), 1) == me
        at = k * chunk
        for s in range(2):
            ins, grads = [], []
            for c in range(2):
                extra = msg[k, s, c, :, wide:].astype(jnp.float32)
                dense_w = extra[:rows, :LANES] + extra[:rows, LANES:] + extra[rows:, :LANES]
                weight = jnp.sum(jnp.where(mine, dense_w, 0.0), axis=1, keepdims=True)
                mask = jnp.sum(jnp.where(mine, extra[rows:, LANES:], 0.0), axis=1, keepdims=True)
                body = msg[k, s, c, :, :wide].astype(jnp.float32)
                ins.append(body[:rows] * mask)
                grads.append(body[rows:] * weight)
                first = at + (2 * s + c) * rows
                scale[first:first + rows, :] = jnp.broadcast_to(weight, (rows, LANES))
            here = slice(at + 2 * s * rows, at + 2 * (s + 1) * rows)
            x_ref[here, :] = jnp.concatenate(ins, axis=0).astype(jnp.bfloat16)
            eg_ref[here, :] = jnp.concatenate(grads, axis=0).astype(jnp.bfloat16)

    def first_half(g, hooks):
        tile = ff
        span = slice(g * held, (g + 1) * held)

        def give(i):
            send(part.at[g, i], other.at[g, i], y_send.at[g, i], y_recv.at[g, i], pair)

        for i, matrix in enumerate((w_gate, w_up)):
            if g == 0:
                loads[4 + i].wait()

            @pl.loop(0, ff // tile)
            def _(n):
                cols = pl.ds(pl.multiple_of(n * tile, tile), tile)
                part[g, i, :, cols] = jnp.dot(
                    x_ref[span, :], matrix[:, cols], preferred_element_type=jnp.float32
                ).astype(jnp.bfloat16)

            give(i)
            for hook in hooks[i]:
                hook()
        if g == 0:
            loads[6].wait()

        @pl.loop(0, ff // tile)
        def _(n):
            cols = pl.ds(pl.multiple_of(n * tile, tile), tile)
            part[g, 2, :, cols] = contract_cols(eg_ref[span, :], w_down[cols, :]).astype(
                jnp.bfloat16
            )

        give(2)
        for hook in hooks[2]:
            hook()

    half = wide // 2
    tile_out = min(512, half)

    def give_back(kind, g, product):
        @pl.loop(0, half // tile_out)
        def _(n):
            cols = pl.ds(pl.multiple_of(n * tile_out, tile_out), tile_out)
            high = pl.ds(pl.multiple_of(half + n * tile_out, tile_out), tile_out)
            left, right = product(cols), product(high)
            for p in range(per):
                for s in range(2):
                    for c in range(2):
                        first = p * chunk + (2 * s + c) * rows
                        block = slice(first, first + rows)
                        back[kind, g, c, s, p, :, cols] = jnp.concatenate(
                            [left[block], right[block]], axis=0
                        ).astype(jnp.bfloat16)

        send(
            back.at[kind, g, 1 - core], back_sib.at[kind, g],
            r1_send.at[kind, g], r1_recv.at[kind, g], sibling,
        )

    def summed(g, i):
        arrived(other.at[g, i], y_send.at[g, i], y_recv.at[g, i], pair)
        return part[g, i].astype(jnp.float32) + other[g, i].astype(jnp.float32)

    def outputs(g):
        span = slice(g * held, (g + 1) * held)
        gate, up_value = summed(g, 0), summed(g, 1)
        hidden_ref[span, :] = (gate * jax.nn.sigmoid(gate) * up_value).astype(jnp.bfloat16)
        give_back(0, g, lambda cols: jnp.dot(
            hidden_ref[span, :], w_down[:, cols], preferred_element_type=jnp.float32
        ) * scale[span, 0:1])

    def inputs(g):
        span = slice(g * held, (g + 1) * held)
        hidden_grad = summed(g, 2)
        gate, up_value = [
            part[g, i].astype(jnp.float32) + other[g, i].astype(jnp.float32) for i in range(2)
        ]
        gg_ref[span, :], ug_ref[span, :] = gate_grads(hidden_grad, gate, up_value)
        give_back(1, g, lambda cols: contract_cols(gg_ref[span, :], w_gate[cols, :])
                  + contract_cols(ug_ref[span, :], w_up[cols, :]))

    def sum_core(kind, g):
        arrived(back_sib.at[kind, g], r1_send.at[kind, g], r1_recv.at[kind, g], sibling)
        mid[kind, g] = (
            back[kind, g, core].astype(jnp.float32) + back_sib[kind, g].astype(jnp.float32)
        ).astype(jnp.bfloat16)
        send(
            mid.at[kind, g, 1 - side], mid_x.at[kind, g],
            r2_send.at[kind, g], r2_recv.at[kind, g], across,
        )

    def sum_side(kind, g):
        arrived(mid_x.at[kind, g], r2_send.at[kind, g], r2_recv.at[kind, g], across)
        last[kind, g] = (
            mid[kind, g, side].astype(jnp.float32) + mid_x[kind, g].astype(jnp.float32)
        ).astype(jnp.bfloat16)
        for p in range(per):
            k = g * per + p
            if k > 0:
                send(
                    last.at[kind, g, p], last_z.at[kind, k],
                    r3_send.at[kind, k], r3_recv.at[kind, k], in_plane(k),
                )

    def finish(kind):
        total = last[kind, 0, 0].astype(jnp.float32)
        for k in range(1, planes):
            arrived(last_z.at[kind, k], r3_send.at[kind, k], r3_recv.at[kind, k], in_plane(k))
            total = total + last_z[kind, k].astype(jnp.float32)
        sum_ref[kind] = total.astype(jnp.bfloat16)

    own = msg.at[0, side, core]
    spread(0)
    for k in range(1, planes):
        send(own, msg.at[k, side, core], z_send.at[k], z_recv.at[k], in_plane(k))

    for k in range(per):
        relay(k)
        if k + 1 < per:
            spread(k + 1)
    for g in range(groups):
        for k in range(g * per, (g + 1) * per):
            gather_end(k)
            gather_rows(k)
        hooks = [[], [], []]
        if g + 1 < groups:
            coming = range((g + 1) * per, (g + 2) * per)
            hooks[0] = [functools.partial(spread, coming[0])]
            hooks[1] = [functools.partial(spread, k) for k in coming[1:]]
            hooks[1].append(functools.partial(relay, coming[0]))
            hooks[2] = [functools.partial(relay, k) for k in coming[1:]]
        first_half(g, hooks)
    step = min(256, wide)

    def down_grad():
        hidden_t = hidden_ref[...].T

        @pl.loop(0, wide // step)
        def _(n):
            cols = pl.ds(pl.multiple_of(n * step, step), step)
            down_ref[:, cols] = jnp.dot(
                hidden_t, eg_ref[:, cols], preferred_element_type=jnp.float32
            ).astype(jnp.bfloat16)

    def in_grads(part_of):
        pieces = wide // step // 2

        @pl.loop(part_of * pieces, (part_of + 1) * pieces)
        def _(n):
            cols = pl.ds(pl.multiple_of(n * step, step), step)
            x_t = x_ref[:, cols].T
            gate_ref[cols, :] = jnp.dot(
                x_t, gg_ref[...], preferred_element_type=jnp.float32
            ).astype(jnp.bfloat16)
            up_ref[cols, :] = jnp.dot(
                x_t, ug_ref[...], preferred_element_type=jnp.float32
            ).astype(jnp.bfloat16)

    for g in range(groups):
        outputs(g)
        if g > 0:
            sum_core(1, g - 1)
            sum_side(0, g - 1)
        inputs(g)
        if g > 0:
            sum_side(1, g - 1)
        sum_core(0, g)
    sum_core(1, groups - 1)
    sum_side(0, groups - 1)
    down_grad()
    sum_side(1, groups - 1)
    in_grads(0)
    in_grads(1)
    finish(0)
    finish(1)
    for copy in sends:
        copy.wait_send()


def exchange(tokens, expert_ids, route_weights, w_gate, w_up, w_down, grad_out):
    rows, wide = tokens.shape
    ff = w_gate.shape[2]
    experts = lax.axis_size("expert")
    planes = experts // 4
    total = experts * rows
    chunk = 4 * rows
    bf16 = jnp.bfloat16
    per = max(1, planes // 2)
    groups = planes // per
    vmem = pl.BlockSpec(memory_space=pltpu.VMEM)
    hbm = pl.BlockSpec(memory_space=pltpu.HBM)
    dma = pltpu.SemaphoreType.DMA
    return pl.pallas_call(
        functools.partial(exchange_kernel, planes, per),
        out_shape=(
            jax.ShapeDtypeStruct((2, 2 * rows, wide // 2), bf16),
            jax.ShapeDtypeStruct((wide, ff), bf16),
            jax.ShapeDtypeStruct((wide, ff), bf16),
            jax.ShapeDtypeStruct((ff, wide), bf16),
        ),
        in_specs=[hbm] * 7,
        out_specs=(vmem,) * 4,
        scratch_shapes=[
            pltpu.VMEM((total, wide), bf16),
            pltpu.VMEM((total, wide), bf16),
            pltpu.VMEM((total, ff), bf16),
            pltpu.VMEM((total, ff), bf16),
            pltpu.VMEM((total, ff), bf16),
            pltpu.VMEM((rows, wide), bf16),
            pltpu.VMEM((rows, wide), bf16),
            pltpu.VMEM(expert_ids.shape, expert_ids.dtype),
            pltpu.VMEM(route_weights.shape, route_weights.dtype),
            pltpu.VMEM((wide, ff), bf16),
            pltpu.VMEM((wide, ff), bf16),
            pltpu.VMEM((ff, wide), bf16),
            dma((7,)),
            pltpu.VMEM((planes, 2, 2, 2 * rows, wide + 2 * LANES), bf16),
            pltpu.VMEM((total, LANES), jnp.float32),
            pltpu.VMEM((groups, 3, per * chunk, ff), bf16),
            pltpu.VMEM((groups, 3, per * chunk, ff), bf16),
            pltpu.VMEM((2, groups, 2, 2, per, 2 * rows, wide // 2), bf16),
            pltpu.VMEM((2, groups, 2, per, 2 * rows, wide // 2), bf16),
            pltpu.VMEM((2, groups, 2, per, 2 * rows, wide // 2), bf16),
            pltpu.VMEM((2, groups, per, 2 * rows, wide // 2), bf16),
            pltpu.VMEM((2, groups, per, 2 * rows, wide // 2), bf16),
            pltpu.VMEM((2, planes, 2 * rows, wide // 2), bf16),
            dma((planes,)), dma((planes,)),
            dma((planes,)), dma((planes,)),
            dma((planes, 2)), dma((planes, 2)),
            dma((groups, 3)), dma((groups, 3)),
            dma((2, groups)), dma((2, groups)),
            dma((2, groups)), dma((2, groups)),
            dma((2, planes)), dma((2, planes)),
        ],
        compiler_params=pltpu.CompilerParams(
            collective_id=0, has_side_effects=True, vmem_limit_bytes=40 * 1024 * 1024
        ),
        name="exchange",
    )(*[
        pltpu.with_memory_space_constraint(operand, pltpu.HBM)
        for operand in (tokens, grad_out, expert_ids, route_weights, w_gate, w_up, w_down)
    ])


PIECES = 4


def store_kernel(sum_ref, gate_in, up_in, down_in,
                 out_ref, in_ref, gate_ref, up_ref, down_ref, sems):
    copies = []
    for i, (source, target) in enumerate(
        ((down_in, down_ref), (gate_in, gate_ref), (up_in, up_ref))
    ):
        size = source.shape[0] // PIECES
        for j in range(PIECES):
            piece = pl.ds(j * size, size)
            copy = pltpu.make_async_copy(source.at[piece], target.at[0, piece], sems.at[i, j])
            copy.start()
            copies.append(copy)
    rows = out_ref.shape[0]
    for kind, ref in enumerate((out_ref, in_ref)):
        both = sum_ref[kind].astype(jnp.float32)
        half = both.shape[1]
        ref[:, :half] = both[:rows].astype(jnp.bfloat16)
        ref[:, half:] = both[rows:].astype(jnp.bfloat16)
    for copy in copies:
        copy.wait()


def store(sums, gate, up, down):
    rows = sums.shape[1] // 2
    wide, ff = gate.shape
    bf16 = jnp.bfloat16
    vmem = pl.BlockSpec(memory_space=pltpu.VMEM)
    anywhere = pl.BlockSpec(memory_space=pl.ANY)
    hbm = pl.BlockSpec(memory_space=pltpu.HBM)
    return pl.pallas_call(
        store_kernel,
        out_shape=(
            jax.ShapeDtypeStruct((rows, wide), bf16),
            jax.ShapeDtypeStruct((rows, wide), bf16),
            jax.ShapeDtypeStruct((1, wide, ff), bf16),
            jax.ShapeDtypeStruct((1, wide, ff), bf16),
            jax.ShapeDtypeStruct((1, ff, wide), bf16),
        ),
        in_specs=[vmem] + [anywhere] * 3,
        out_specs=(vmem, vmem, hbm, hbm, hbm),
        scratch_shapes=[pltpu.SemaphoreType.DMA((3, PIECES))],
        compiler_params=pltpu.CompilerParams(vmem_limit_bytes=16 * 1024 * 1024),
        name="store",
    )(sums, gate, up, down)


def local(tokens, expert_ids, route_weights, w_gate, w_up, w_down, grad_out):
    experts = lax.axis_size("expert")
    planes = experts // 4
    fits = (
        lax.axis_size("dp") == 2
        and experts % 4 == 0
        and planes & (planes - 1) == 0
        and planes <= 4
        and experts <= LANES
        and tokens.shape[0] % 8 == 0
    )
    if not fits:
        return general(tokens, expert_ids, route_weights, w_gate, w_up, w_down, grad_out)
    return store(
        *exchange(tokens, expert_ids, route_weights, w_gate, w_up, w_down, grad_out)
    )


def solution(mesh):
    return jax.shard_map(
        local,
        mesh=mesh,
        in_specs=(
            P("expert", "dp"),
            P("expert", None),
            P("expert", None),
            P("expert", "dp", None),
            P("expert", "dp", None),
            P("expert", None, "dp"),
            P("expert", "dp"),
        ),
        out_specs=(
            P("expert", "dp"),
            P("expert", "dp"),
            P("expert", "dp", None),
            P("expert", "dp", None),
            P("expert", None, "dp"),
        ),
        check_vma=False,
    )
```

```python
import functools

import jax
import jax.numpy as jnp
from jax import lax
from jax.experimental import pallas as pl
from jax.experimental.pallas import tpu as pltpu
from jax.sharding import PartitionSpec as P

MESH = pl.DeviceIdType.MESH
LANES = 128


def slot_table(id_block, experts, capacity):
    flat_ids = id_block.reshape(-1)
    onehot = (flat_ids[:, None] == jnp.arange(experts, dtype=jnp.int32)[None, :]).astype(jnp.int32)
    before = jnp.cumsum(onehot, axis=0) - onehot
    slot_index = jnp.sum(before * onehot, axis=1)
    target = flat_ids * capacity + slot_index
    row_index = jnp.arange(experts * capacity, dtype=jnp.int32)
    return (row_index[:, None] == target[None, :]).astype(jnp.bfloat16)


def gate_grads(hidden_grad, gate, up_value):
    sigmoid_gate = jax.nn.sigmoid(gate)
    silu_gate = gate * sigmoid_gate
    gate_grad = (
        hidden_grad * up_value * sigmoid_gate * (1.0 + gate * (1.0 - sigmoid_gate))
    ).astype(jnp.bfloat16)
    up_grad = (hidden_grad * silu_gate).astype(jnp.bfloat16)
    return (gate_grad, up_grad)


def contract_rows(left, right):
    return lax.dot_general(
        left, right, (((0,), (0,)), ((), ())), preferred_element_type=jnp.float32
    )


def contract_cols(left, right):
    return lax.dot_general(
        left, right, (((1,), (1,)), ((), ())), preferred_element_type=jnp.float32
    )


def general(tokens, expert_ids, route_weights, w_gate, w_up, w_down, grad_out):
    tok_rows = tokens.shape[0]
    slices = tokens.shape[1]
    top_count = expert_ids.shape[1]
    experts = lax.axis_size("expert")
    capacity = min(tok_rows, 3 * tok_rows * top_count // experts)
    table = slot_table(expert_ids, experts, capacity)
    weight_flat = route_weights.reshape(-1)
    token_replicas = jnp.repeat(tokens, top_count, axis=0)
    grad_rep = (
        jnp.repeat(grad_out, top_count, axis=0).astype(jnp.float32) * weight_flat[:, None]
    ).astype(jnp.bfloat16)
    dispatch_token_rows = jnp.dot(table, token_replicas, preferred_element_type=jnp.float32).astype(
        jnp.bfloat16
    )
    dispatch_gradients = jnp.dot(table, grad_rep, preferred_element_type=jnp.float32).astype(
        jnp.bfloat16
    )
    dispatch_token_rows = dispatch_token_rows.reshape(experts, capacity, slices)
    dispatch_gradients = dispatch_gradients.reshape(experts, capacity, slices)
    expert_in, expert_grad = (
        lax.all_to_all(dispatch_token_rows, "expert", split_axis=0, concat_axis=0, tiled=True),
        lax.all_to_all(dispatch_gradients, "expert", split_axis=0, concat_axis=0, tiled=True),
    )
    expert_in = expert_in.reshape(-1, slices)
    expert_grad = expert_grad.reshape(-1, slices)
    gate_matrix = w_gate[0]
    up_matrix = w_up[0]
    down_matrix = w_down[0]
    gate_part = jnp.dot(expert_in, gate_matrix, preferred_element_type=jnp.float32)
    up_part = jnp.dot(expert_in, up_matrix, preferred_element_type=jnp.float32)
    gate, up_value = (
        lax.psum(gate_part.astype(jnp.bfloat16), "dp").astype(jnp.float32),
        lax.psum(up_part.astype(jnp.bfloat16), "dp").astype(jnp.float32),
    )
    hidden = (gate * jax.nn.sigmoid(gate) * up_value).astype(jnp.bfloat16)
    expert_out = jnp.dot(hidden, down_matrix, preferred_element_type=jnp.float32).astype(
        jnp.bfloat16
    )
    out_blocks = expert_out.reshape(experts, capacity, slices)
    grad_part = contract_cols(expert_grad, down_matrix)
    hidden_grad = lax.psum(grad_part.astype(jnp.bfloat16), "dp").astype(jnp.float32)
    gate_grad, up_grad = gate_grads(hidden_grad, gate, up_value)
    down_grad = contract_rows(hidden, expert_grad).astype(jnp.bfloat16)
    gate_weight = contract_rows(expert_in, gate_grad).astype(jnp.bfloat16)
    up_weight = contract_rows(expert_in, up_grad).astype(jnp.bfloat16)
    input_rows = (contract_cols(gate_grad, gate_matrix) + contract_cols(up_grad, up_matrix)).astype(
        jnp.bfloat16
    )
    input_blocks = input_rows.reshape(experts, capacity, slices)
    out_back, input_back = (
        lax.all_to_all(out_blocks, "expert", split_axis=0, concat_axis=0, tiled=True),
        lax.all_to_all(input_blocks, "expert", split_axis=0, concat_axis=0, tiled=True),
    )
    backward_output = contract_rows(table, out_back.reshape(-1, slices)).reshape(
        tok_rows, top_count, slices
    )
    backward_input = contract_rows(table, input_back.reshape(-1, slices)).reshape(
        tok_rows, top_count, slices
    )
    layer_out = jnp.sum(backward_output * route_weights[:, :, None], axis=1).astype(jnp.bfloat16)
    input_grad = jnp.sum(backward_input, axis=1).astype(jnp.bfloat16)
    return (layer_out, input_grad, gate_weight[None], up_weight[None], down_grad[None])


def partner(index, step):
    bit = 1
    while bit <= step:
        if step & bit:
            index = index + bit - 2 * bit * ((index // bit) % 2)
        bit *= 2
    return index


def exchange_kernel(
    planes, per,
    tok_hbm, grad_hbm, id_hbm, weight_hbm, gate_hbm, up_hbm, down_hbm,
    sum_ref, gate_ref, up_ref, down_ref,
    x_ref, eg_ref, hidden_ref, gg_ref, ug_ref,
    tok_ref, grad_ref, id_ref, weight_ref,
    w_gate, w_up, w_down, load_sem,
    msg, scale, part, other, back, back_sib, mid, mid_x, last, last_z,
    z_send, z_recv, x_send, x_recv, s_send, s_recv, y_send, y_recv,
    r1_send, r1_recv, r2_send, r2_recv, r3_send, r3_recv,
):
    rows, wide = tok_ref.shape
    ff = w_gate.shape[1]
    top = id_ref.shape[1]
    chunk = 4 * rows
    groups = planes // per
    held = per * chunk
    me = lax.axis_index("expert")
    core = me % 2
    side = (me // 2) % 2
    plane = me // 4
    pair = {"dp": 1 - lax.axis_index("dp")}
    sibling = {"expert": plane * 4 + side * 2 + (1 - core)}
    across = {"expert": plane * 4 + (1 - side) * 2 + core}

    def in_plane(step):
        return {"expert": partner(plane, step) * 4 + side * 2 + core}

    loads = []
    for i, (source, target) in enumerate((
        (tok_hbm, tok_ref), (grad_hbm, grad_ref), (id_hbm, id_ref), (weight_hbm, weight_ref),
        (gate_hbm.at[0], w_gate), (up_hbm.at[0], w_up), (down_hbm.at[0], w_down),
    )):
        load = pltpu.make_async_copy(source, target, load_sem.at[i])
        load.start()
        loads.append(load)

    peers = [sibling, across, pair] + [in_plane(step) for step in range(1, planes)]
    barrier = pltpu.get_barrier_semaphore()
    for peer in peers:
        pl.semaphore_signal(barrier, inc=1, device_id=peer, device_id_type=MESH)

    for load in loads[:4]:
        load.wait()
    half = wide // 2
    lane = lax.broadcasted_iota(jnp.int32, (rows, LANES), 1)
    dense = jnp.zeros((rows, LANES), jnp.float32)
    chosen = jnp.zeros((rows, LANES), jnp.float32)
    for k in range(top):
        hit = id_ref[:, k:k + 1] == lane % (LANES // 2)
        dense = dense + jnp.where(hit, weight_ref[:, k:k + 1], 0.0)
        chosen = chosen + jnp.where(hit, 1.0, 0.0)
    high = dense.astype(jnp.bfloat16).astype(jnp.float32)
    middle = (dense - high).astype(jnp.bfloat16).astype(jnp.float32)
    low = dense - high - middle
    extras = (
        (chosen, jnp.zeros_like(chosen)),
        (jnp.where(lane < LANES // 2, high, middle), low),
    )
    for kind, ref in enumerate((tok_ref, grad_ref)):
        body = ref[...].astype(jnp.float32)
        msg[kind, 0, side, core, :, :half] = jnp.concatenate(
            [body[:, :half], body[:, half:]], axis=0
        ).astype(jnp.bfloat16)
        msg[kind, 0, side, core, :, half:] = jnp.concatenate(
            extras[kind], axis=0
        ).astype(jnp.bfloat16)

    pl.semaphore_wait(barrier, len(peers))

    sends = []

    def send(source, target, send_sem, recv_sem, device):
        copy = pltpu.make_async_remote_copy(
            src_ref=source, dst_ref=target, send_sem=send_sem, recv_sem=recv_sem,
            device_id=device, device_id_type=MESH,
        )
        copy.start()
        sends.append(copy)

    def arrived(target, send_sem, recv_sem, device):
        pltpu.make_async_remote_copy(
            src_ref=target, dst_ref=target, send_sem=send_sem, recv_sem=recv_sem,
            device_id=device, device_id_type=MESH,
        ).wait_recv()

    def spread(kind, k):
        own = msg.at[kind, k, side, core]
        if k > 0:
            arrived(own, z_send.at[kind, k], z_recv.at[kind, k], in_plane(k))
        send(own, own, x_send.at[kind, k], x_recv.at[kind, k], across)
        send(own, own, s_send.at[kind, k, 0], s_recv.at[kind, k, 0], sibling)

    def relay(kind, k):
        far = msg.at[kind, k, 1 - side, core]
        arrived(far, x_send.at[kind, k], x_recv.at[kind, k], across)
        send(far, far, s_send.at[kind, k, 1], s_recv.at[kind, k, 1], sibling)

    def gather(kind, k):
        for i, s in enumerate((side, 1 - side)):
            arrived(
                msg.at[kind, k, s, 1 - core],
                s_send.at[kind, k, i], s_recv.at[kind, k, i], sibling,
            )
        place = lax.broadcasted_iota(jnp.int32, (rows, LANES), 1)
        at = k * chunk
        target = (x_ref, eg_ref)[kind]
        for s in range(2):
            left, right = [], []
            for c in range(2):
                extra = msg[kind, k, s, c, :, half:].astype(jnp.float32)
                if kind == 0:
                    kept = jnp.where(place == me, extra[:rows], 0.0)
                else:
                    kept = jnp.where(place % (LANES // 2) == me, extra[:rows], 0.0)
                    kept = kept + jnp.where(place == me, extra[rows:], 0.0)
                factor = jnp.sum(kept, axis=1, keepdims=True)
                body = msg[kind, k, s, c, :, :half].astype(jnp.float32)
                left.append(body[:rows] * factor)
                right.append(body[rows:] * factor)
                if kind == 1:
                    first = at + (2 * s + c) * rows
                    scale[first:first + rows, :] = jnp.broadcast_to(factor, (rows, LANES))
            here = slice(at + 2 * s * rows, at + 2 * (s + 1) * rows)
            target[here, :half] = jnp.concatenate(left, axis=0).astype(jnp.bfloat16)
            target[here, half:] = jnp.concatenate(right, axis=0).astype(jnp.bfloat16)

    def first_half(g, hooks):
        tile = ff
        span = slice(g * held, (g + 1) * held)

        def give(i):
            send(part.at[g, i], other.at[g, i], y_send.at[g, i], y_recv.at[g, i], pair)

        for i, matrix in enumerate((w_gate, w_up)):
            if g == 0:
                loads[4 + i].wait()

            @pl.loop(0, ff // tile)
            def _(n):
                cols = pl.ds(pl.multiple_of(n * tile, tile), tile)
                part[g, i, :, cols] = jnp.dot(
                    x_ref[span, :], matrix[:, cols], preferred_element_type=jnp.float32
                ).astype(jnp.bfloat16)

            give(i)
            for hook in hooks[i]:
                hook()
        for k in range(g * per, (g + 1) * per):
            gather(1, k)
        if g == 0:
            loads[6].wait()

        @pl.loop(0, ff // tile)
        def _(n):
            cols = pl.ds(pl.multiple_of(n * tile, tile), tile)
            part[g, 2, :, cols] = contract_cols(eg_ref[span, :], w_down[cols, :]).astype(
                jnp.bfloat16
            )

        give(2)
        for hook in hooks[2]:
            hook()

    tile_out = min(512, half)

    def give_back(kind, g, product):
        @pl.loop(0, half // tile_out)
        def _(n):
            cols = pl.ds(pl.multiple_of(n * tile_out, tile_out), tile_out)
            high = pl.ds(pl.multiple_of(half + n * tile_out, tile_out), tile_out)
            left, right = product(cols), product(high)
            for p in range(per):
                for s in range(2):
                    for c in range(2):
                        first = p * chunk + (2 * s + c) * rows
                        block = slice(first, first + rows)
                        back[kind, g, c, s, p, :, cols] = jnp.concatenate(
                            [left[block], right[block]], axis=0
                        ).astype(jnp.bfloat16)

        send(
            back.at[kind, g, 1 - core], back_sib.at[kind, g],
            r1_send.at[kind, g], r1_recv.at[kind, g], sibling,
        )

    def summed(g, i):
        arrived(other.at[g, i], y_send.at[g, i], y_recv.at[g, i], pair)
        return part[g, i].astype(jnp.float32) + other[g, i].astype(jnp.float32)

    def outputs(g):
        span = slice(g * held, (g + 1) * held)
        gate, up_value = summed(g, 0), summed(g, 1)
        hidden_ref[span, :] = (gate * jax.nn.sigmoid(gate) * up_value).astype(jnp.bfloat16)
        give_back(0, g, lambda cols: jnp.dot(
            hidden_ref[span, :], w_down[:, cols], preferred_element_type=jnp.float32
        ) * scale[span, 0:1])

    def inputs(g):
        span = slice(g * held, (g + 1) * held)
        hidden_grad = summed(g, 2)
        gate, up_value = [
            part[g, i].astype(jnp.float32) + other[g, i].astype(jnp.float32) for i in range(2)
        ]
        gg_ref[span, :], ug_ref[span, :] = gate_grads(hidden_grad, gate, up_value)
        give_back(1, g, lambda cols: contract_cols(gg_ref[span, :], w_gate[cols, :])
                  + contract_cols(ug_ref[span, :], w_up[cols, :]))

    def sum_core(kind, g):
        arrived(back_sib.at[kind, g], r1_send.at[kind, g], r1_recv.at[kind, g], sibling)
        mid[kind, g] = (
            back[kind, g, core].astype(jnp.float32) + back_sib[kind, g].astype(jnp.float32)
        ).astype(jnp.bfloat16)
        send(
            mid.at[kind, g, 1 - side], mid_x.at[kind, g],
            r2_send.at[kind, g], r2_recv.at[kind, g], across,
        )

    def sum_side(kind, g):
        arrived(mid_x.at[kind, g], r2_send.at[kind, g], r2_recv.at[kind, g], across)
        last[kind, g] = (
            mid[kind, g, side].astype(jnp.float32) + mid_x[kind, g].astype(jnp.float32)
        ).astype(jnp.bfloat16)
        for p in range(per):
            k = g * per + p
            if k > 0:
                send(
                    last.at[kind, g, p], last_z.at[kind, k],
                    r3_send.at[kind, k], r3_recv.at[kind, k], in_plane(k),
                )

    def finish(kind):
        total = last[kind, 0, 0].astype(jnp.float32)
        for k in range(1, planes):
            arrived(last_z.at[kind, k], r3_send.at[kind, k], r3_recv.at[kind, k], in_plane(k))
            total = total + last_z[kind, k].astype(jnp.float32)
        sum_ref[kind] = total.astype(jnp.bfloat16)

    for k in range(planes):
        for kind in range(2):
            if k == 0:
                spread(kind, 0)
            else:
                send(
                    msg.at[kind, 0, side, core], msg.at[kind, k, side, core],
                    z_send.at[kind, k], z_recv.at[kind, k], in_plane(k),
                )
    for k in range(per):
        relay(0, k)
        if k + 1 < per:
            spread(0, k + 1)
    for g in range(groups):
        now = range(g * per, (g + 1) * per)
        coming = range((g + 1) * per, (g + 2) * per) if g + 1 < groups else ()
        for k in now:
            gather(0, k)
        hooks = [[], [], []]
        if g == 0:
            for k in now:
                hooks[0].append(functools.partial(relay, 1, k))
                if k + 1 < per:
                    hooks[0].append(functools.partial(spread, 1, k + 1))
        else:
            hooks[0] += [functools.partial(relay, 1, k) for k in now]
        for k in coming:
            hooks[1].append(functools.partial(spread, 0, k))
        for k in coming:
            hooks[2].append(functools.partial(relay, 0, k))
            hooks[2].append(functools.partial(spread, 1, k))
        first_half(g, hooks)

    step = min(256, wide)

    def down_grad():
        hidden_t = hidden_ref[...].T

        @pl.loop(0, wide // step)
        def _(n):
            cols = pl.ds(pl.multiple_of(n * step, step), step)
            down_ref[:, cols] = jnp.dot(
                hidden_t, eg_ref[:, cols], preferred_element_type=jnp.float32
            ).astype(jnp.bfloat16)

    def in_grads(part_of):
        pieces = wide // step // 2

        @pl.loop(part_of * pieces, (part_of + 1) * pieces)
        def _(n):
            cols = pl.ds(pl.multiple_of(n * step, step), step)
            x_t = x_ref[:, cols].T
            gate_ref[cols, :] = jnp.dot(
                x_t, gg_ref[...], preferred_element_type=jnp.float32
            ).astype(jnp.bfloat16)
            up_ref[cols, :] = jnp.dot(
                x_t, ug_ref[...], preferred_element_type=jnp.float32
            ).astype(jnp.bfloat16)

    for g in range(groups):
        outputs(g)
        if g > 0:
            sum_core(1, g - 1)
            sum_side(0, g - 1)
        inputs(g)
        if g > 0:
            sum_side(1, g - 1)
        sum_core(0, g)
    sum_core(1, groups - 1)
    sum_side(0, groups - 1)
    down_grad()
    sum_side(1, groups - 1)
    in_grads(0)
    in_grads(1)
    finish(0)
    finish(1)
    for copy in sends:
        copy.wait_send()


def exchange(tokens, expert_ids, route_weights, w_gate, w_up, w_down, grad_out):
    rows, wide = tokens.shape
    ff = w_gate.shape[2]
    experts = lax.axis_size("expert")
    planes = experts // 4
    total = experts * rows
    chunk = 4 * rows
    bf16 = jnp.bfloat16
    per = max(1, planes // 2)
    groups = planes // per
    vmem = pl.BlockSpec(memory_space=pltpu.VMEM)
    hbm = pl.BlockSpec(memory_space=pltpu.HBM)
    dma = pltpu.SemaphoreType.DMA
    return pl.pallas_call(
        functools.partial(exchange_kernel, planes, per),
        out_shape=(
            jax.ShapeDtypeStruct((2, 2 * rows, wide // 2), bf16),
            jax.ShapeDtypeStruct((wide, ff), bf16),
            jax.ShapeDtypeStruct((wide, ff), bf16),
            jax.ShapeDtypeStruct((ff, wide), bf16),
        ),
        in_specs=[hbm] * 7,
        out_specs=(vmem,) * 4,
        scratch_shapes=[
            pltpu.VMEM((total, wide), bf16),
            pltpu.VMEM((total, wide), bf16),
            pltpu.VMEM((total, ff), bf16),
            pltpu.VMEM((total, ff), bf16),
            pltpu.VMEM((total, ff), bf16),
            pltpu.VMEM((rows, wide), bf16),
            pltpu.VMEM((rows, wide), bf16),
            pltpu.VMEM(expert_ids.shape, expert_ids.dtype),
            pltpu.VMEM(route_weights.shape, route_weights.dtype),
            pltpu.VMEM((wide, ff), bf16),
            pltpu.VMEM((wide, ff), bf16),
            pltpu.VMEM((ff, wide), bf16),
            dma((7,)),
            pltpu.VMEM((2, planes, 2, 2, 2 * rows, wide // 2 + LANES), bf16),
            pltpu.VMEM((total, LANES), jnp.float32),
            pltpu.VMEM((groups, 3, per * chunk, ff), bf16),
            pltpu.VMEM((groups, 3, per * chunk, ff), bf16),
            pltpu.VMEM((2, groups, 2, 2, per, 2 * rows, wide // 2), bf16),
            pltpu.VMEM((2, groups, 2, per, 2 * rows, wide // 2), bf16),
            pltpu.VMEM((2, groups, 2, per, 2 * rows, wide // 2), bf16),
            pltpu.VMEM((2, groups, per, 2 * rows, wide // 2), bf16),
            pltpu.VMEM((2, groups, per, 2 * rows, wide // 2), bf16),
            pltpu.VMEM((2, planes, 2 * rows, wide // 2), bf16),
            dma((2, planes)), dma((2, planes)),
            dma((2, planes)), dma((2, planes)),
            dma((2, planes, 2)), dma((2, planes, 2)),
            dma((groups, 3)), dma((groups, 3)),
            dma((2, groups)), dma((2, groups)),
            dma((2, groups)), dma((2, groups)),
            dma((2, planes)), dma((2, planes)),
        ],
        compiler_params=pltpu.CompilerParams(
            collective_id=0, has_side_effects=True, vmem_limit_bytes=40 * 1024 * 1024
        ),
        name="exchange",
    )(*[
        pltpu.with_memory_space_constraint(operand, pltpu.HBM)
        for operand in (tokens, grad_out, expert_ids, route_weights, w_gate, w_up, w_down)
    ])


PIECES = 4


def store_kernel(sum_ref, gate_in, up_in, down_in,
                 out_ref, in_ref, gate_ref, up_ref, down_ref, sems):
    copies = []
    for i, (source, target) in enumerate(
        ((down_in, down_ref), (gate_in, gate_ref), (up_in, up_ref))
    ):
        size = source.shape[0] // PIECES
        for j in range(PIECES):
            piece = pl.ds(j * size, size)
            copy = pltpu.make_async_copy(source.at[piece], target.at[0, piece], sems.at[i, j])
            copy.start()
            copies.append(copy)
    rows = out_ref.shape[0]
    for kind, ref in enumerate((out_ref, in_ref)):
        both = sum_ref[kind].astype(jnp.float32)
        half = both.shape[1]
        ref[:, :half] = both[:rows].astype(jnp.bfloat16)
        ref[:, half:] = both[rows:].astype(jnp.bfloat16)
    for copy in copies:
        copy.wait()


def store(sums, gate, up, down):
    rows = sums.shape[1] // 2
    wide, ff = gate.shape
    bf16 = jnp.bfloat16
    vmem = pl.BlockSpec(memory_space=pltpu.VMEM)
    anywhere = pl.BlockSpec(memory_space=pl.ANY)
    hbm = pl.BlockSpec(memory_space=pltpu.HBM)
    return pl.pallas_call(
        store_kernel,
        out_shape=(
            jax.ShapeDtypeStruct((rows, wide), bf16),
            jax.ShapeDtypeStruct((rows, wide), bf16),
            jax.ShapeDtypeStruct((1, wide, ff), bf16),
            jax.ShapeDtypeStruct((1, wide, ff), bf16),
            jax.ShapeDtypeStruct((1, ff, wide), bf16),
        ),
        in_specs=[vmem] + [anywhere] * 3,
        out_specs=(vmem, vmem, hbm, hbm, hbm),
        scratch_shapes=[pltpu.SemaphoreType.DMA((3, PIECES))],
        compiler_params=pltpu.CompilerParams(vmem_limit_bytes=16 * 1024 * 1024),
        name="store",
    )(sums, gate, up, down)


def local(tokens, expert_ids, route_weights, w_gate, w_up, w_down, grad_out):
    experts = lax.axis_size("expert")
    planes = experts // 4
    fits = (
        lax.axis_size("dp") == 2
        and experts % 4 == 0
        and planes & (planes - 1) == 0
        and planes <= 4
        and experts <= LANES // 2
        and tokens.shape[0] % 8 == 0
    )
    if not fits:
        return general(tokens, expert_ids, route_weights, w_gate, w_up, w_down, grad_out)
    return store(
        *exchange(tokens, expert_ids, route_weights, w_gate, w_up, w_down, grad_out)
    )


def solution(mesh):
    return jax.shard_map(
        local,
        mesh=mesh,
        in_specs=(
            P("expert", "dp"),
            P("expert", None),
            P("expert", None),
            P("expert", "dp", None),
            P("expert", "dp", None),
            P("expert", None, "dp"),
            P("expert", "dp"),
        ),
        out_specs=(
            P("expert", "dp"),
            P("expert", "dp"),
            P("expert", "dp", None),
            P("expert", "dp", None),
            P("expert", None, "dp"),
        ),
        check_vma=False,
    )
```

```python
import functools

import jax
import jax.numpy as jnp
from jax import lax
from jax.experimental import pallas as pl
from jax.experimental.pallas import tpu as pltpu
from jax.sharding import PartitionSpec as P

MESH = pl.DeviceIdType.MESH
LANES = 128


def slot_table(id_block, experts, capacity):
    flat_ids = id_block.reshape(-1)
    onehot = (flat_ids[:, None] == jnp.arange(experts, dtype=jnp.int32)[None, :]).astype(jnp.int32)
    before = jnp.cumsum(onehot, axis=0) - onehot
    slot_index = jnp.sum(before * onehot, axis=1)
    target = flat_ids * capacity + slot_index
    row_index = jnp.arange(experts * capacity, dtype=jnp.int32)
    return (row_index[:, None] == target[None, :]).astype(jnp.bfloat16)


def gate_grads(hidden_grad, gate, up_value):
    sigmoid_gate = jax.nn.sigmoid(gate)
    silu_gate = gate * sigmoid_gate
    gate_grad = (
        hidden_grad * up_value * sigmoid_gate * (1.0 + gate * (1.0 - sigmoid_gate))
    ).astype(jnp.bfloat16)
    up_grad = (hidden_grad * silu_gate).astype(jnp.bfloat16)
    return (gate_grad, up_grad)


def contract_rows(left, right):
    return lax.dot_general(
        left, right, (((0,), (0,)), ((), ())), preferred_element_type=jnp.float32
    )


def contract_cols(left, right):
    return lax.dot_general(
        left, right, (((1,), (1,)), ((), ())), preferred_element_type=jnp.float32
    )


def general(tokens, expert_ids, route_weights, w_gate, w_up, w_down, grad_out):
    tok_rows = tokens.shape[0]
    slices = tokens.shape[1]
    top_count = expert_ids.shape[1]
    experts = lax.axis_size("expert")
    capacity = min(tok_rows, 3 * tok_rows * top_count // experts)
    table = slot_table(expert_ids, experts, capacity)
    weight_flat = route_weights.reshape(-1)
    token_replicas = jnp.repeat(tokens, top_count, axis=0)
    grad_rep = (
        jnp.repeat(grad_out, top_count, axis=0).astype(jnp.float32) * weight_flat[:, None]
    ).astype(jnp.bfloat16)
    dispatch_token_rows = jnp.dot(table, token_replicas, preferred_element_type=jnp.float32).astype(
        jnp.bfloat16
    )
    dispatch_gradients = jnp.dot(table, grad_rep, preferred_element_type=jnp.float32).astype(
        jnp.bfloat16
    )
    dispatch_token_rows = dispatch_token_rows.reshape(experts, capacity, slices)
    dispatch_gradients = dispatch_gradients.reshape(experts, capacity, slices)
    expert_in, expert_grad = (
        lax.all_to_all(dispatch_token_rows, "expert", split_axis=0, concat_axis=0, tiled=True),
        lax.all_to_all(dispatch_gradients, "expert", split_axis=0, concat_axis=0, tiled=True),
    )
    expert_in = expert_in.reshape(-1, slices)
    expert_grad = expert_grad.reshape(-1, slices)
    gate_matrix = w_gate[0]
    up_matrix = w_up[0]
    down_matrix = w_down[0]
    gate_part = jnp.dot(expert_in, gate_matrix, preferred_element_type=jnp.float32)
    up_part = jnp.dot(expert_in, up_matrix, preferred_element_type=jnp.float32)
    gate, up_value = (
        lax.psum(gate_part.astype(jnp.bfloat16), "dp").astype(jnp.float32),
        lax.psum(up_part.astype(jnp.bfloat16), "dp").astype(jnp.float32),
    )
    hidden = (gate * jax.nn.sigmoid(gate) * up_value).astype(jnp.bfloat16)
    expert_out = jnp.dot(hidden, down_matrix, preferred_element_type=jnp.float32).astype(
        jnp.bfloat16
    )
    out_blocks = expert_out.reshape(experts, capacity, slices)
    grad_part = contract_cols(expert_grad, down_matrix)
    hidden_grad = lax.psum(grad_part.astype(jnp.bfloat16), "dp").astype(jnp.float32)
    gate_grad, up_grad = gate_grads(hidden_grad, gate, up_value)
    down_grad = contract_rows(hidden, expert_grad).astype(jnp.bfloat16)
    gate_weight = contract_rows(expert_in, gate_grad).astype(jnp.bfloat16)
    up_weight = contract_rows(expert_in, up_grad).astype(jnp.bfloat16)
    input_rows = (contract_cols(gate_grad, gate_matrix) + contract_cols(up_grad, up_matrix)).astype(
        jnp.bfloat16
    )
    input_blocks = input_rows.reshape(experts, capacity, slices)
    out_back, input_back = (
        lax.all_to_all(out_blocks, "expert", split_axis=0, concat_axis=0, tiled=True),
        lax.all_to_all(input_blocks, "expert", split_axis=0, concat_axis=0, tiled=True),
    )
    backward_output = contract_rows(table, out_back.reshape(-1, slices)).reshape(
        tok_rows, top_count, slices
    )
    backward_input = contract_rows(table, input_back.reshape(-1, slices)).reshape(
        tok_rows, top_count, slices
    )
    layer_out = jnp.sum(backward_output * route_weights[:, :, None], axis=1).astype(jnp.bfloat16)
    input_grad = jnp.sum(backward_input, axis=1).astype(jnp.bfloat16)
    return (layer_out, input_grad, gate_weight[None], up_weight[None], down_grad[None])


def partner(index, step):
    bit = 1
    while bit <= step:
        if step & bit:
            index = index + bit - 2 * bit * ((index // bit) % 2)
        bit *= 2
    return index


def exchange_kernel(
    planes, per,
    tok_hbm, grad_hbm, id_hbm, weight_hbm, gate_hbm, up_hbm, down_hbm,
    sum_ref, gate_ref, up_ref, down_ref,
    x_ref, eg_ref, hidden_ref, gg_ref, ug_ref,
    tok_ref, grad_ref, id_ref, weight_ref,
    w_gate, w_up, w_down, load_sem,
    msg, scale, part, other, back, back_sib, mid, mid_x, last, last_z,
    z_send, z_recv, x_send, x_recv, s_send, s_recv, y_send, y_recv,
    r1_send, r1_recv, r2_send, r2_recv, r3_send, r3_recv,
):
    rows, wide = tok_ref.shape
    ff = w_gate.shape[1]
    top = id_ref.shape[1]
    chunk = 4 * rows
    groups = planes // per
    held = per * chunk
    me = lax.axis_index("expert")
    core = me % 2
    side = (me // 2) % 2
    plane = me // 4
    pair = {"dp": 1 - lax.axis_index("dp")}
    sibling = {"expert": plane * 4 + side * 2 + (1 - core)}
    across = {"expert": plane * 4 + (1 - side) * 2 + core}

    def in_plane(step):
        return {"expert": partner(plane, step) * 4 + side * 2 + core}

    loads = []
    for i, (source, target) in enumerate((
        (tok_hbm, tok_ref), (grad_hbm, grad_ref), (id_hbm, id_ref), (weight_hbm, weight_ref),
        (gate_hbm.at[0], w_gate), (up_hbm.at[0], w_up), (down_hbm.at[0], w_down),
    )):
        load = pltpu.make_async_copy(source, target, load_sem.at[i])
        load.start()
        loads.append(load)

    peers = [sibling, across, pair] + [in_plane(step) for step in range(1, planes)]
    barrier = pltpu.get_barrier_semaphore()
    for peer in peers:
        pl.semaphore_signal(barrier, inc=1, device_id=peer, device_id_type=MESH)

    for load in loads[:4]:
        load.wait()
    lane = lax.broadcasted_iota(jnp.int32, (rows, LANES), 1)
    dense = jnp.zeros((rows, LANES), jnp.float32)
    chosen = jnp.zeros((rows, LANES), jnp.float32)
    for k in range(top):
        hit = id_ref[:, k:k + 1] == lane
        dense = dense + jnp.where(hit, weight_ref[:, k:k + 1], 0.0)
        chosen = chosen + jnp.where(hit, 1.0, 0.0)
    high = dense.astype(jnp.bfloat16).astype(jnp.float32)
    middle = (dense - high).astype(jnp.bfloat16).astype(jnp.float32)
    low = dense - high - middle
    both = jnp.concatenate(
        [tok_ref[...].astype(jnp.float32), grad_ref[...].astype(jnp.float32)], axis=0
    )
    extra_a = jnp.concatenate([high, low], axis=0)
    extra_b = jnp.concatenate([middle, chosen], axis=0)
    msg[0, side, core, :, :wide] = both.astype(jnp.bfloat16)
    msg[0, side, core, :, wide:wide + LANES] = extra_a.astype(jnp.bfloat16)
    msg[0, side, core, :, wide + LANES:] = extra_b.astype(jnp.bfloat16)

    pl.semaphore_wait(barrier, len(peers))

    sends = []

    def send(source, target, send_sem, recv_sem, device):
        copy = pltpu.make_async_remote_copy(
            src_ref=source, dst_ref=target, send_sem=send_sem, recv_sem=recv_sem,
            device_id=device, device_id_type=MESH,
        )
        copy.start()
        sends.append(copy)

    def arrived(target, send_sem, recv_sem, device):
        pltpu.make_async_remote_copy(
            src_ref=target, dst_ref=target, send_sem=send_sem, recv_sem=recv_sem,
            device_id=device, device_id_type=MESH,
        ).wait_recv()

    def spread(k):
        own = msg.at[k, side, core]
        if k > 0:
            arrived(own, z_send.at[k], z_recv.at[k], in_plane(k))
        send(own, own, x_send.at[k], x_recv.at[k], across)
        send(own, own, s_send.at[k, 0], s_recv.at[k, 0], sibling)

    def relay(k):
        far = msg.at[k, 1 - side, core]
        arrived(far, x_send.at[k], x_recv.at[k], across)
        send(far, far, s_send.at[k, 1], s_recv.at[k, 1], sibling)

    def gather_end(k):
        arrived(msg.at[k, side, 1 - core], s_send.at[k, 0], s_recv.at[k, 0], sibling)
        arrived(msg.at[k, 1 - side, 1 - core], s_send.at[k, 1], s_recv.at[k, 1], sibling)

    def gather_rows(k):
        mine = lax.broadcasted_iota(jnp.int32, (rows, LANES), 1) == me
        at = k * chunk
        for s in range(2):
            ins, grads = [], []
            for c in range(2):
                extra = msg[k, s, c, :, wide:].astype(jnp.float32)
                dense_w = extra[:rows, :LANES] + extra[:rows, LANES:] + extra[rows:, :LANES]
                weight = jnp.sum(jnp.where(mine, dense_w, 0.0), axis=1, keepdims=True)
                mask = jnp.sum(jnp.where(mine, extra[rows:, LANES:], 0.0), axis=1, keepdims=True)
                body = msg[k, s, c, :, :wide].astype(jnp.float32)
                ins.append(body[:rows] * mask)
                grads.append(body[rows:] * weight)
                first = at + (2 * s + c) * rows
                scale[first:first + rows, :] = jnp.broadcast_to(weight, (rows, LANES))
            here = slice(at + 2 * s * rows, at + 2 * (s + 1) * rows)
            x_ref[here, :] = jnp.concatenate(ins, axis=0).astype(jnp.bfloat16)
            eg_ref[here, :] = jnp.concatenate(grads, axis=0).astype(jnp.bfloat16)

    def first_half(g, hooks):
        tile = ff
        span = slice(g * held, (g + 1) * held)

        def give(i):
            send(part.at[g, i], other.at[g, i], y_send.at[g, i], y_recv.at[g, i], pair)

        for i, matrix in enumerate((w_gate, w_up)):
            if g == 0:
                loads[4 + i].wait()

            @pl.loop(0, ff // tile)
            def _(n):
                cols = pl.ds(pl.multiple_of(n * tile, tile), tile)
                part[g, i, :, cols] = jnp.dot(
                    x_ref[span, :], matrix[:, cols], preferred_element_type=jnp.float32
                ).astype(jnp.bfloat16)

            give(i)
            for hook in hooks[i]:
                hook()
        if g == 0:
            loads[6].wait()

        @pl.loop(0, ff // tile)
        def _(n):
            cols = pl.ds(pl.multiple_of(n * tile, tile), tile)
            part[g, 2, :, cols] = contract_cols(eg_ref[span, :], w_down[cols, :]).astype(
                jnp.bfloat16
            )

        give(2)
        for hook in hooks[2]:
            hook()

    half = wide // 2
    tile_out = min(512, half)

    def give_back(kind, g, product):
        @pl.loop(0, half // tile_out)
        def _(n):
            cols = pl.ds(pl.multiple_of(n * tile_out, tile_out), tile_out)
            high = pl.ds(pl.multiple_of(half + n * tile_out, tile_out), tile_out)
            left, right = product(cols), product(high)
            for p in range(per):
                for s in range(2):
                    for c in range(2):
                        first = p * chunk + (2 * s + c) * rows
                        block = slice(first, first + rows)
                        back[kind, g, c, s, p, :, cols] = jnp.concatenate(
                            [left[block], right[block]], axis=0
                        ).astype(jnp.bfloat16)

        send(
            back.at[kind, g, 1 - core], back_sib.at[kind, g],
            r1_send.at[kind, g], r1_recv.at[kind, g], sibling,
        )

    def summed(g, i):
        arrived(other.at[g, i], y_send.at[g, i], y_recv.at[g, i], pair)
        return part[g, i].astype(jnp.float32) + other[g, i].astype(jnp.float32)

    def outputs(g):
        span = slice(g * held, (g + 1) * held)
        gate, up_value = summed(g, 0), summed(g, 1)
        hidden_ref[span, :] = (gate * jax.nn.sigmoid(gate) * up_value).astype(jnp.bfloat16)
        give_back(0, g, lambda cols: jnp.dot(
            hidden_ref[span, :], w_down[:, cols], preferred_element_type=jnp.float32
        ) * scale[span, 0:1])

    def inputs(g):
        span = slice(g * held, (g + 1) * held)
        hidden_grad = summed(g, 2)
        gate, up_value = [
            part[g, i].astype(jnp.float32) + other[g, i].astype(jnp.float32) for i in range(2)
        ]
        gg_ref[span, :], ug_ref[span, :] = gate_grads(hidden_grad, gate, up_value)
        give_back(1, g, lambda cols: contract_cols(gg_ref[span, :], w_gate[cols, :])
                  + contract_cols(ug_ref[span, :], w_up[cols, :]))

    def sum_core(kind, g):
        arrived(back_sib.at[kind, g], r1_send.at[kind, g], r1_recv.at[kind, g], sibling)
        mid[kind, g] = (
            back[kind, g, core].astype(jnp.float32) + back_sib[kind, g].astype(jnp.float32)
        ).astype(jnp.bfloat16)
        send(
            mid.at[kind, g, 1 - side], mid_x.at[kind, g],
            r2_send.at[kind, g], r2_recv.at[kind, g], across,
        )

    def sum_side(kind, g):
        arrived(mid_x.at[kind, g], r2_send.at[kind, g], r2_recv.at[kind, g], across)
        last[kind, g] = (
            mid[kind, g, side].astype(jnp.float32) + mid_x[kind, g].astype(jnp.float32)
        ).astype(jnp.bfloat16)
        for p in range(per):
            k = g * per + p
            if k > 0:
                send(
                    last.at[kind, g, p], last_z.at[kind, k],
                    r3_send.at[kind, k], r3_recv.at[kind, k], in_plane(k),
                )

    def finish(kind):
        total = last[kind, 0, 0].astype(jnp.float32)
        for k in range(1, planes):
            arrived(last_z.at[kind, k], r3_send.at[kind, k], r3_recv.at[kind, k], in_plane(k))
            total = total + last_z[kind, k].astype(jnp.float32)
        sum_ref[kind] = total.astype(jnp.bfloat16)

    own = msg.at[0, side, core]
    spread(0)
    for k in range(1, planes):
        send(own, msg.at[k, side, core], z_send.at[k], z_recv.at[k], in_plane(k))

    if per > 1:
        spread(1)
    for k in range(per):
        relay(k)
        if k + 2 < per:
            spread(k + 2)
    for g in range(groups):
        for k in range(g * per, (g + 1) * per):
            gather_end(k)
            gather_rows(k)
        hooks = [[], [], []]
        if g + 1 < groups:
            coming = range((g + 1) * per, (g + 2) * per)
            hooks[0] = [functools.partial(spread, coming[0])]
            hooks[1] = [functools.partial(spread, k) for k in coming[1:]]
            hooks[1].append(functools.partial(relay, coming[0]))
            hooks[2] = [functools.partial(relay, k) for k in coming[1:]]
        first_half(g, hooks)
    step = min(256, wide)

    def down_grad():
        hidden_t = hidden_ref[...].T

        @pl.loop(0, wide // step)
        def _(n):
            cols = pl.ds(pl.multiple_of(n * step, step), step)
            down_ref[:, cols] = jnp.dot(
                hidden_t, eg_ref[:, cols], preferred_element_type=jnp.float32
            ).astype(jnp.bfloat16)

    def in_grads(part_of):
        pieces = wide // step // 2

        @pl.loop(part_of * pieces, (part_of + 1) * pieces)
        def _(n):
            cols = pl.ds(pl.multiple_of(n * step, step), step)
            x_t = x_ref[:, cols].T
            gate_ref[cols, :] = jnp.dot(
                x_t, gg_ref[...], preferred_element_type=jnp.float32
            ).astype(jnp.bfloat16)
            up_ref[cols, :] = jnp.dot(
                x_t, ug_ref[...], preferred_element_type=jnp.float32
            ).astype(jnp.bfloat16)

    for g in range(groups):
        outputs(g)
        if g == groups - 1 and g == 0:
            sum_core(0, g)
        if g > 0:
            sum_core(1, g - 1)
            sum_side(0, g - 1)
        if g == groups - 1:
            down_grad()
        inputs(g)
        if g > 0:
            sum_side(1, g - 1)
        if groups > 1:
            sum_core(0, g)
    sum_core(1, groups - 1)
    sum_side(0, groups - 1)
    in_grads(0)
    sum_side(1, groups - 1)
    in_grads(1)
    finish(0)
    finish(1)
    for copy in sends:
        copy.wait_send()


def exchange(tokens, expert_ids, route_weights, w_gate, w_up, w_down, grad_out):
    rows, wide = tokens.shape
    ff = w_gate.shape[2]
    experts = lax.axis_size("expert")
    planes = experts // 4
    total = experts * rows
    chunk = 4 * rows
    bf16 = jnp.bfloat16
    per = planes
    groups = planes // per
    vmem = pl.BlockSpec(memory_space=pltpu.VMEM)
    hbm = pl.BlockSpec(memory_space=pltpu.HBM)
    dma = pltpu.SemaphoreType.DMA
    return pl.pallas_call(
        functools.partial(exchange_kernel, planes, per),
        out_shape=(
            jax.ShapeDtypeStruct((2, 2 * rows, wide // 2), bf16),
            jax.ShapeDtypeStruct((wide, ff), bf16),
            jax.ShapeDtypeStruct((wide, ff), bf16),
            jax.ShapeDtypeStruct((ff, wide), bf16),
        ),
        in_specs=[hbm] * 7,
        out_specs=(vmem,) * 4,
        scratch_shapes=[
            pltpu.VMEM((total, wide), bf16),
            pltpu.VMEM((total, wide), bf16),
            pltpu.VMEM((total, ff), bf16),
            pltpu.VMEM((total, ff), bf16),
            pltpu.VMEM((total, ff), bf16),
            pltpu.VMEM((rows, wide), bf16),
            pltpu.VMEM((rows, wide), bf16),
            pltpu.VMEM(expert_ids.shape, expert_ids.dtype),
            pltpu.VMEM(route_weights.shape, route_weights.dtype),
            pltpu.VMEM((wide, ff), bf16),
            pltpu.VMEM((wide, ff), bf16),
            pltpu.VMEM((ff, wide), bf16),
            dma((7,)),
            pltpu.VMEM((planes, 2, 2, 2 * rows, wide + 2 * LANES), bf16),
            pltpu.VMEM((total, LANES), jnp.float32),
            pltpu.VMEM((groups, 3, per * chunk, ff), bf16),
            pltpu.VMEM((groups, 3, per * chunk, ff), bf16),
            pltpu.VMEM((2, groups, 2, 2, per, 2 * rows, wide // 2), bf16),
            pltpu.VMEM((2, groups, 2, per, 2 * rows, wide // 2), bf16),
            pltpu.VMEM((2, groups, 2, per, 2 * rows, wide // 2), bf16),
            pltpu.VMEM((2, groups, per, 2 * rows, wide // 2), bf16),
            pltpu.VMEM((2, groups, per, 2 * rows, wide // 2), bf16),
            pltpu.VMEM((2, planes, 2 * rows, wide // 2), bf16),
            dma((planes,)), dma((planes,)),
            dma((planes,)), dma((planes,)),
            dma((planes, 2)), dma((planes, 2)),
            dma((groups, 3)), dma((groups, 3)),
            dma((2, groups)), dma((2, groups)),
            dma((2, groups)), dma((2, groups)),
            dma((2, planes)), dma((2, planes)),
        ],
        compiler_params=pltpu.CompilerParams(
            collective_id=0, has_side_effects=True, vmem_limit_bytes=40 * 1024 * 1024
        ),
        name="exchange",
    )(*[
        pltpu.with_memory_space_constraint(operand, pltpu.HBM)
        for operand in (tokens, grad_out, expert_ids, route_weights, w_gate, w_up, w_down)
    ])


PIECES = 4


def store_kernel(sum_ref, gate_in, up_in, down_in,
                 out_ref, in_ref, gate_ref, up_ref, down_ref, sems):
    copies = []
    for i, (source, target) in enumerate(
        ((down_in, down_ref), (gate_in, gate_ref), (up_in, up_ref))
    ):
        size = source.shape[0] // PIECES
        for j in range(PIECES):
            piece = pl.ds(j * size, size)
            copy = pltpu.make_async_copy(source.at[piece], target.at[0, piece], sems.at[i, j])
            copy.start()
            copies.append(copy)
    rows = out_ref.shape[0]
    for kind, ref in enumerate((out_ref, in_ref)):
        both = sum_ref[kind].astype(jnp.float32)
        half = both.shape[1]
        ref[:, :half] = both[:rows].astype(jnp.bfloat16)
        ref[:, half:] = both[rows:].astype(jnp.bfloat16)
    for copy in copies:
        copy.wait()


def store(sums, gate, up, down):
    rows = sums.shape[1] // 2
    wide, ff = gate.shape
    bf16 = jnp.bfloat16
    vmem = pl.BlockSpec(memory_space=pltpu.VMEM)
    anywhere = pl.BlockSpec(memory_space=pl.ANY)
    hbm = pl.BlockSpec(memory_space=pltpu.HBM)
    return pl.pallas_call(
        store_kernel,
        out_shape=(
            jax.ShapeDtypeStruct((rows, wide), bf16),
            jax.ShapeDtypeStruct((rows, wide), bf16),
            jax.ShapeDtypeStruct((1, wide, ff), bf16),
            jax.ShapeDtypeStruct((1, wide, ff), bf16),
            jax.ShapeDtypeStruct((1, ff, wide), bf16),
        ),
        in_specs=[vmem] + [anywhere] * 3,
        out_specs=(vmem, vmem, hbm, hbm, hbm),
        scratch_shapes=[pltpu.SemaphoreType.DMA((3, PIECES))],
        compiler_params=pltpu.CompilerParams(vmem_limit_bytes=16 * 1024 * 1024),
        name="store",
    )(sums, gate, up, down)


def local(tokens, expert_ids, route_weights, w_gate, w_up, w_down, grad_out):
    experts = lax.axis_size("expert")
    planes = experts // 4
    fits = (
        lax.axis_size("dp") == 2
        and experts % 4 == 0
        and planes & (planes - 1) == 0
        and planes <= 4
        and experts <= LANES
        and tokens.shape[0] % 8 == 0
    )
    if not fits:
        return general(tokens, expert_ids, route_weights, w_gate, w_up, w_down, grad_out)
    return store(
        *exchange(tokens, expert_ids, route_weights, w_gate, w_up, w_down, grad_out)
    )


def solution(mesh):
    return jax.shard_map(
        local,
        mesh=mesh,
        in_specs=(
            P("expert", "dp"),
            P("expert", None),
            P("expert", None),
            P("expert", "dp", None),
            P("expert", "dp", None),
            P("expert", None, "dp"),
            P("expert", "dp"),
        ),
        out_specs=(
            P("expert", "dp"),
            P("expert", "dp"),
            P("expert", "dp", None),
            P("expert", "dp", None),
            P("expert", None, "dp"),
        ),
        check_vma=False,
    )
```
